32 devices in a mesh: gx: 4 (over x, core), gy: 8 (over z, y).
Axes of the slice: x: 2, y: 2, z: 4, core: 2. Of those that a mesh axis runs over, the one named last changes fastest.
Arguments:
- populations: float32 [19, 64, 128, 128], P(None, 'gx', 'gy'), may hold values from 0.02 to 0.1
- porosity: float32 [64, 128, 128], P('gx', 'gy'), may hold values from 0.05 to 0.95
- adjoint_in: float32 [19, 64, 128, 128], P(None, 'gx', 'gy'), may hold values from -6 to 6
- porous: int32 [64, 128, 128], P('gx', 'gy'), may hold values 0 or 1
- walls: int32 [64, 128, 128], P('gx', 'gy'), may hold values 0 or 1
- owners: int32 [4, 8, 64, 1], P('gx', 'gy'), may hold values from 0 to 31; in each aligned block of 64 rows (0 to 63, 64 to 127, ..., all dimensions but the last counted through in order) at most 4 rows name the same one
- slots: int32 [4, 8, 64], P('gx', 'gy'), may hold values from 0 to 255
Outputs:
- adjoint_out: float32 [19, 64, 128, 128], P(None, 'gx', 'gy')
- patch_sens: float32 [8192], P(('gx', 'gy'))
The draws below stay inside these ranges and needn't reach their ends.
Inputs may be any that keep to these rules, and one draw needn't show every extreme that they name: `owners`: of the 64 panel blocks of one device, at most 4 name the same owner device, and some device's blocks reach 4 for some owner in every draw.
All inputs are finite; a program needn't handle non-finite values. No bound on the sum of `porous` or of `walls` on one device may be relied on, other than what follows from the above.
Results may differ from the reference program's by a relative error of at most 0.0003.
Values sent between devices are 32-bit elements; how exact they have to be, the bound alone decides.
A program may use at most 128 MiB of HBM per device.

```python
import math
from functools import partial
import jax
import jax.numpy as jnp
import numpy as np
from jax import lax

Q = 19
CX = 16
CY = 16
NZ = 128
BLOCK = 2
PATCH_DEV = 256
NX = 64
NY = 128
BLK_DEV = 64
CAP = 4
PATCHES = 8192
N_GX = 4
N_GY = 8
DEVICES = 32


def plant(drawn, stream_key, low, top_value):
    shape = drawn.shape
    place = [jax.random.randint(jax.random.fold_in(stream_key, axis), (), 0, shape[axis]) for axis in range(len(shape))]
    drawn = drawn.at[tuple(place)].set(low)
    longest = shape.index(max(shape))
    place[longest] = (place[longest] + 1) % shape[longest]
    return drawn.at[tuple(place)].set(top_value)


def levels(key, extent, split, low, top_value):
    def one(dim, parts):
        heights = jax.random.uniform(jax.random.fold_in(jax.random.fold_in(key, 6), dim), (parts,), jnp.float32, low / len(split), top_value / len(split))
        return jnp.repeat(jnp.exp(heights), extent[dim] // parts).reshape((-1,) + (1,) * (len(extent) - dim - 1))

    gain = one(*split[0])
    for cut in split[1:]:
        gain = gain * one(*cut)
    return gain


def assign_block(stream_key, own, number, rows, number_of, top, bound, slope):
    ranking = jax.random.permutation(stream_key, number_of)
    heavy_load, usual = portions_of(number_of, rows * top, bound, slope, True), portions_of(number_of, rows * top, bound, slope, False)
    places = jnp.arange(number_of)

    def named(lengths, turn):
        used = int((lengths > 0).sum())
        fixed = max(1, used // 4)
        moved = fixed + (places - fixed + turn * (used - fixed)) % max(1, number_of - fixed)
        return jnp.zeros((number_of,), jnp.int32).at[ranking[jnp.where(places < fixed, places, moved)]].set(jnp.asarray(lengths, jnp.int32))

    lengths = jnp.where(number % 4 == 0, named(heavy_load, number // 4), named(usual, number - number // 4 - 1))
    mixed = jax.random.permutation(jax.random.fold_in(own, 3), number_of)
    source_of, taker = mixed[0:number_of // 2 * 2:2], mixed[1:number_of // 2 * 2:2]
    slack = jnp.minimum(lengths[source_of] - 1, bound - lengths[taker]) // 2
    slack = jnp.where((source_of == ranking[0]) | (taker == ranking[0]) | (lengths[taker] == 0), 0, jnp.maximum(slack, 0))
    moved = jax.random.randint(jax.random.fold_in(own, 4), (number_of // 2,), 0, 1 << 20) % (slack + 1)
    lengths = lengths.at[source_of].add(-moved).at[taker].add(moved)
    members = jnp.searchsorted(jnp.cumsum(lengths), jnp.arange(rows * top), side="right").astype(jnp.int32)
    grid = members.reshape(top, rows).T
    grid = grid[jax.random.permutation(jax.random.fold_in(own, 1), rows)]
    turn = jax.random.randint(jax.random.fold_in(own, 2), (rows, 1), 0, top)
    return jnp.take_along_axis(grid, (jnp.arange(top)[None, :] + turn) % top, axis=1)


def portions_of(number_of, total, limit, lean, full):
    loads = [(1 << 20) // math.isqrt(rank ** lean) + 1 for rank in range(1, number_of + 1)]
    largest = limit if full else min(limit, max(-(-total // number_of), total * loads[0] // sum(loads)))
    least = 1 if total - largest >= number_of - 1 else 0
    given, spare = [largest] + [least] * (number_of - 1), total - largest - least * (number_of - 1)
    while spare > 0:
        movable = [i for i in range(1, number_of) if given[i] < largest] or [i for i in range(1, number_of) if given[i] < limit]
        mass, remaining = sum([loads[i] for i in movable]), spare
        for i in movable:
            more = min(limit - given[i], max(1, remaining * loads[i] // mass), spare)
            given[i] = given[i] + more
            spare = spare - more
    return np.array(given)


def scatter_about(key, shape, scale, limit, pieces=(), kind=jnp.bfloat16):
    loudness = levels(key, shape, pieces, -0.22, 0.18) if pieces else 1.0
    values = jax.random.normal(key, shape, jnp.float32) * scale * loudness
    return jnp.minimum(jnp.maximum(values, -limit), limit).astype(kind)


def setup_inputs(seed: int = 0) -> dict:
    splits = jax.random.split(jax.random.key(seed), 8)
    populations = jnp.clip(0.02 + 0.08 * jax.random.uniform(splits[0], (Q, NX, NY, NZ), jnp.float32) ** levels(splits[0], (Q, NX, NY, NZ), ((1, 4), (2, 8)), -0.2, 0.2), 0.02, 0.1)
    porosity = jnp.clip(0.05 + 0.9 * jax.random.uniform(splits[1], (NX, NY, NZ), jnp.float32) ** levels(splits[1], (NX, NY, NZ), ((0, 4), (1, 8)), -0.2, 0.2), 0.05, 0.95)
    adjoint_in = scatter_about(splits[2], (Q, NX, NY, NZ), 1.0, 6.0, ((1, 4), (2, 8)), jnp.float32)
    porous = plant((jax.random.randint(splits[3], (NX, NY, NZ), 0, 2) < 1).astype(jnp.int32), jax.random.fold_in(splits[3], 1), 0, 1)
    walls = plant((jax.random.randint(splits[4], (NX, NY, NZ), 0, 8) < 1).astype(jnp.int32), jax.random.fold_in(splits[4], 1), 0, 1)
    owners_keys = jax.random.split(jax.random.fold_in(splits[5], 1), N_GX * N_GY * BLK_DEV // BLK_DEV)
    owners_turns = jax.random.permutation(jax.random.fold_in(splits[5], 3), N_GX * N_GY * BLK_DEV // BLK_DEV)
    owners = jax.vmap(lambda own, number: assign_block(jax.random.fold_in(splits[5], 2), own, number, BLK_DEV, DEVICES, 1, CAP, 2))(owners_keys, owners_turns).reshape((N_GX, N_GY, BLK_DEV, 1))
    slots = plant(jax.random.randint(splits[6], (N_GX, N_GY, BLK_DEV), 0, PATCH_DEV), jax.random.fold_in(splits[6], 1), 0, PATCH_DEV - 1).astype(jnp.int32)
    return {"populations": populations, "porosity": porosity, "adjoint_in": adjoint_in, "porous": porous, "walls": walls, "owners": owners, "slots": slots}


velocities = [[0, 0, 0], [1, 0, 0], [-1, 0, 0], [0, 1, 0], [0, -1, 0], [0, 0, 1], [0, 0, -1], [1, 1, 0], [-1, -1, 0], [1, -1, 0], [-1, 1, 0], [1, 0, 1], [-1, 0, -1], [1, 0, -1], [-1, 0, 1], [0, 1, 1], [0, -1, -1], [0, 1, -1], [0, -1, 1]]
opposite = [0, 2, 1, 4, 3, 6, 5, 8, 7, 10, 9, 12, 11, 14, 13, 16, 15, 18, 17]
lattice_weights = [1.0 / 3.0] + [1.0 / 18.0] * 6 + [1.0 / 36.0] * 12
moment_powers = [[0, 0, 0], [1, 0, 0], [0, 1, 0], [0, 0, 1], [2, 0, 0], [0, 2, 0], [0, 0, 2], [1, 1, 0], [0, 1, 1], [1, 0, 1], [2, 1, 0], [2, 0, 1], [1, 2, 0], [0, 2, 1], [1, 0, 2], [0, 1, 2], [2, 2, 0], [0, 2, 2], [2, 0, 2]]
relax_rates = [0.0] * 4 + [1.25] * 6 + [1.5] * 6 + [1.4] * 3

def invert_table(matrix):
    order = len(matrix)
    table = [list(matrix[row_index]) + [1.0 if row_index == other else 0.0 for other in range(order)] for row_index in range(order)]
    for column in range(order):
        pivot_row = max(range(column, order), key=lambda candidate: abs(table[candidate][column]))
        table[column], table[pivot_row] = (table[pivot_row], table[column])
        leading = table[column][column]
        table[column] = [entry / leading for entry in table[column]]
        for row_index in range(order):
            if row_index != column:
                factor = table[row_index][column]
                table[row_index] = [first - factor * second for first, second in zip(table[row_index], table[column])]
    return [row[order:] for row in table]

def relaxation():
    moments = [[float(vector[0] ** power[0] * vector[1] ** power[1] * vector[2] ** power[2]) for vector in velocities] for power in moment_powers]
    inverse = invert_table(moments)
    return [[sum((inverse[row_index][middle] * relax_rates[middle] * moments[middle][column] for middle in range(19))) for column in range(19)] for row_index in range(19)]

def collide(populations, porosity, porous, walls):
    highest = lax.Precision.HIGHEST
    vectors = jnp.asarray(velocities, dtype=jnp.float32)
    weights = jnp.asarray(lattice_weights, dtype=jnp.float32)
    kernel = jnp.asarray(relaxation(), dtype=jnp.float32)
    density = lax.optimization_barrier(jnp.sum(populations, axis=0))
    momentum = jnp.einsum('iq,ixyz->qxyz', vectors, populations, precision=highest)
    velocity = momentum / density
    projected = jnp.einsum('iq,qxyz->ixyz', vectors, velocity, precision=highest)
    speed_square = lax.optimization_barrier(jnp.sum(velocity * velocity, axis=0))
    equilibrium = weights[:, None, None, None] * density * (1.0 + 3.0 * projected + 4.5 * projected * projected - 1.5 * speed_square)
    relaxed = populations - jnp.einsum('ij,jxyz->ixyz', kernel, populations - equilibrium, precision=highest)
    fraction = jnp.where(walls == 1, jnp.float32(1.0), porous.astype(jnp.float32) * porosity)
    reversed_pop = jnp.stack([populations[index] for index in opposite])
    return (1.0 - fraction) * relaxed + fraction * reversed_pop

def stream(field, direction):
    moved = []
    for lattice_dir in range(19):
        offsets = tuple((int(direction * value) for value in velocities[lattice_dir]))
        moved.append(jnp.roll(field[lattice_dir], offsets, axis=(0, 1, 2)))
    return jnp.stack(moved)

def reference(populations, porosity, adjoint_in, porous, walls, owners, slots):
    collide_here = partial(collide, porous=porous, walls=walls)
    read = stream(collide_here(populations, porosity), 1)
    _, pull_late = jax.vjp(collide_here, read, porosity)
    late_adjoint, late_sens = pull_late(adjoint_in)
    pulled = stream(late_adjoint, -1)
    _, pull_early = jax.vjp(collide_here, populations, porosity)
    adjoint_out, early_sens = pull_early(pulled)
    node_sens = early_sens + late_sens
    blocks = lax.optimization_barrier(jnp.sum(node_sens.reshape(NX // BLOCK, BLOCK, NY // BLOCK, BLOCK, NZ), axis=(1, 3, 4)))
    blocks = blocks.reshape(N_GX, CX // BLOCK, N_GY, CY // BLOCK).transpose(0, 2, 1, 3).reshape(-1)
    patch_ids = (owners.reshape(-1) * PATCH_DEV + slots.reshape(-1)).astype(jnp.int32)
    patch_sens = jax.ops.segment_sum(blocks, patch_ids, num_segments=PATCHES)
    return (adjoint_out, patch_sens)
```

```python
from functools import partial

import jax
import jax.numpy as jnp
from jax import lax
from jax.experimental import pallas as pl
from jax.experimental.pallas import tpu as pltpu
from jax.sharding import PartitionSpec as P

PATCH_DEV = 256
MESH = pl.DeviceIdType.MESH

VELOCITIES = [
    (0, 0, 0),
    (1, 0, 0), (-1, 0, 0), (0, 1, 0), (0, -1, 0), (0, 0, 1), (0, 0, -1),
    (1, 1, 0), (-1, -1, 0), (1, -1, 0), (-1, 1, 0),
    (1, 0, 1), (-1, 0, -1), (1, 0, -1), (-1, 0, 1),
    (0, 1, 1), (0, -1, -1), (0, 1, -1), (0, -1, 1),
]
ORDER = [0, 3, 4, 5, 6, 15, 16, 17, 18, 1, 7, 9, 11, 13, 2, 8, 10, 12, 14]
POS = [ORDER.index(i) for i in range(19)]
X_START = {1: 9, -1: 14}
Y_GROUP = {1: [3, 7, 10, 15, 17], -1: [4, 8, 9, 16, 18]}
CORNERS = [(1, 1), (-1, -1), (1, -1), (-1, 1)]
CORNER_POP = {(1, 1): 7, (-1, -1): 8, (1, -1): 9, (-1, 1): 10}
PLANES = (7, 11, 15)
RATE2, RATE3, RATE4 = 1.25, 1.5, 1.4


def split_planes(f):
    out = []
    for start in PLANES:
        a, b, c, d = f[start : start + 4]
        s1, s2, t1, t2 = a + b, c + d, a - b, c - d
        out.append((s1 + s2, s1 - s2, t1 + t2, t1 - t2, t1, t2))
    return out


def split_faces(f):
    return [f[1] + f[2], f[3] + f[4], f[5] + f[6]], [f[1] - f[2], f[3] - f[4], f[5] - f[6]]


def nonequilibrium(f):
    (w_xy, w_xz, w_yz) = planes = split_planes(f)
    sums, diffs = split_faces(f)
    second = [sums[0] + w_xy[0] + w_xz[0], sums[1] + w_xy[0] + w_yz[0], sums[2] + w_xz[0] + w_yz[0]]
    jx = diffs[0] + (w_xy[2] + w_xz[2])
    jy = diffs[1] + (w_xy[3] + w_yz[2])
    jz = diffs[2] + (w_xz[3] + w_yz[3])
    rho = (f[0] + sums[0]) + (sums[1] + sums[2]) + ((w_xy[0] + w_xz[0]) + w_yz[0])
    inverse = 1.0 / rho
    ux, uy, uz = jx * inverse, jy * inverse, jz * inverse
    qx, qy, qz = jx * ux, jy * uy, jz * uz
    third_rho = rho * (1.0 / 3.0)
    second = [second[0] - third_rho - qx, second[1] - third_rho - qy, second[2] - third_rho - qz]
    product = [w_xy[1] - jx * uy, w_xz[1] - jx * uz, w_yz[1] - jy * uz]
    kx, ky, kz = jx * (1.0 / 3.0), jy * (1.0 / 3.0), jz * (1.0 / 3.0)
    first = [w_xy[2] - kx, w_xz[2] - kx, w_yz[2] - ky]
    other = [w_xy[3] - ky, w_xz[3] - kz, w_yz[3] - kz]
    base = rho * (1.0 / 9.0) + ((qx + qy) + qz) * (1.0 / 3.0)
    fourth = [w_xy[0] - base + 0.5 * qz, w_xz[0] - base + 0.5 * qy, w_yz[0] - base + 0.5 * qx]
    return planes, diffs, (ux, uy, uz), (second, product, first, other, fourth)


def forward(f, phi):
    _, _, _, (second, product, first, other, fourth) = nonequilibrium(f)
    second = [v * (0.5 * RATE2) for v in second]
    product = [v * (0.25 * RATE2) for v in product]
    first = [v * (0.25 * RATE3) for v in first]
    other = [v * (0.25 * RATE3) for v in other]
    fourth = [v * (0.25 * RATE4) for v in fourth]
    change = [None] * 19
    change[0] = 4.0 * (fourth[0] + fourth[1] + fourth[2]) - 2.0 * (second[0] + second[1] + second[2])
    evens = [
        second[0] - 2.0 * (fourth[0] + fourth[1]),
        second[1] - 2.0 * (fourth[0] + fourth[2]),
        second[2] - 2.0 * (fourth[1] + fourth[2]),
    ]
    odds = [
        2.0 * (first[0] + first[1]),
        2.0 * (other[0] + first[2]),
        2.0 * (other[1] + other[2]),
    ]
    for axis in range(3):
        change[1 + 2 * axis] = evens[axis] - odds[axis]
        change[2 + 2 * axis] = evens[axis] + odds[axis]
    for plane, start in enumerate(PLANES):
        h, k = fourth[plane] + product[plane], fourth[plane] - product[plane]
        p, q = first[plane] + other[plane], first[plane] - other[plane]
        change[start : start + 4] = [h + p, h - p, k + q, k - q]
    relaxed = [f[i] - change[i] for i in range(19)]
    opposite = [0] + [i + 1 if i % 2 else i - 1 for i in range(1, 19)]
    return [relaxed[i] + phi * (f[opposite[i]] - relaxed[i]) for i in range(19)]


def backward(f, a, phi):
    f_planes, f_diffs, (ux, uy, uz), moments = nonequilibrium(f)
    a_planes = split_planes(a)
    a_sums, a_diffs = split_faces(a)
    half = [0.5 * v for v in a_sums]
    n_xy, n_xz, n_yz = a_planes
    b2 = [RATE2 * (v - a[0]) for v in half]
    b11 = [(0.25 * RATE2) * n[1] for n in a_planes]
    hx, hy, hz = [(0.5 * RATE3) * v for v in a_diffs]
    b_first = [
        (0.25 * RATE3) * n_xy[2] - hx, (0.25 * RATE3) * n_xz[2] - hx, (0.25 * RATE3) * n_yz[2] - hy
    ]
    b_other = [
        (0.25 * RATE3) * n_xy[3] - hy, (0.25 * RATE3) * n_xz[3] - hz, (0.25 * RATE3) * n_yz[3] - hz
    ]
    b4 = [
        RATE4 * (0.25 * n_xy[0] - (half[0] + half[1]) + a[0]),
        RATE4 * (0.25 * n_xz[0] - (half[0] + half[2]) + a[0]),
        RATE4 * (0.25 * n_yz[0] - (half[1] + half[2]) + a[0]),
    ]
    sens = None
    for mine, theirs in zip((b2, b11, b_first, b_other, b4), moments):
        for v, m in zip(mine, theirs):
            sens = v * m if sens is None else sens + v * m
    for axis in range(3):
        sens = sens - f_diffs[axis] * a_diffs[axis]
    for p, n in zip(f_planes, a_planes):
        sens = sens - p[4] * n[4] - p[5] * n[5]

    keep = 1.0 - phi
    b2, b11, b_first, b_other, b4 = [
        [keep * v for v in part] for part in (b2, b11, b_first, b_other, b4)
    ]
    total4 = b4[0] + b4[1] + b4[2]
    twice = total4 * (2.0 / 3.0)
    cx, cy, cz = 2.0 * b2[0] + twice - b4[2], 2.0 * b2[1] + twice - b4[1], 2.0 * b2[2] + twice - b4[0]
    wx = cx * ux + b11[0] * uy + b11[1] * uz
    wy = cy * uy + b11[0] * ux + b11[2] * uz
    wz = cz * uz + b11[1] * ux + b11[2] * uy
    r0 = (
        0.5 * (ux * wx + uy * wy + uz * wz)
        - (b2[0] + b2[1] + b2[2]) * (1.0 / 3.0)
        - total4 * (1.0 / 9.0)
    )
    rx = -(b_first[0] + b_first[1]) * (1.0 / 3.0) - wx
    ry = -(b_other[0] + b_first[2]) * (1.0 / 3.0) - wy
    rz = -(b_other[1] + b_other[2]) * (1.0 / 3.0) - wz
    result = [None] * 19
    result[0] = a[0] - r0
    evens = [r0 + b2[0], r0 + b2[1], r0 + b2[2]]
    for axis, odd in enumerate((rx, ry, rz)):
        back = phi * a_diffs[axis] + odd
        result[1 + 2 * axis] = (a[1 + 2 * axis] - evens[axis]) - back
        result[2 + 2 * axis] = (a[2 + 2 * axis] - evens[axis]) + back
    for plane, (start, one, two) in enumerate(((7, 0, 1), (11, 0, 2), (15, 1, 2))):
        even = evens[one] + b2[two] + b4[plane]
        p = (rx, ry, rz)[one] + b_first[plane]
        q = (rx, ry, rz)[two] + b_other[plane]
        h, k = even + b11[plane], even - b11[plane]
        s = (p + q) + phi * a_planes[plane][4]
        t = (p - q) + phi * a_planes[plane][5]
        result[start] = (a[start] - h) - s
        result[start + 1] = (a[start + 1] - h) + s
        result[start + 2] = (a[start + 2] - k) - t
        result[start + 3] = (a[start + 3] - k) + t
    return result, sens


def kernel(
    sizes, pops_hbm, porosity_hbm, adj_hbm, porous_hbm, walls_hbm, ids_ref, out_hbm, patch_ref,
    pops, porosity, adj, porous, walls, out, ahead, behind, late_sens, early_sens,
    y_send, y_recv, c_send, c_recv, message, gathered,
    load_sem, store_sem, halo_send, halo_recv, patch_send, patch_recv,
):
    n_gx, n_gy, cx, cy, nz = sizes
    n = n_gx * n_gy
    stride = cy + 16
    gx, gy = lax.axis_index("gx"), lax.axis_index("gy")
    me = gx * n_gy + gy

    loads = [
        pltpu.make_async_copy(src, dst, load_sem.at[k])
        for k, (src, dst) in enumerate((
            (porosity_hbm, porosity), (porous_hbm, porous), (walls_hbm, walls),
            (pops_hbm, pops), (adj_hbm, adj),
        ))
    ]
    for load in loads:
        load.start()

    def place(k):
        index = lax.rem(me + k, n)
        return (index // n_gy, lax.rem(index, n_gy))

    barrier = pltpu.get_barrier_semaphore()

    @pl.loop(1, n)
    def _(k):
        pl.semaphore_signal(barrier, inc=1, device_id=place(k), device_id_type=MESH)

    def near(dx, dy):
        return (lax.rem(gx + (dx + n_gx), n_gx), lax.rem(gy + (dy + n_gy), n_gy))

    def spin(value, shift):
        return value if shift == 0 else pltpu.roll(value, shift % nz, 1)

    def window(x, y, along_x):
        return pl.ds(x * cy + y, 8, stride=cy) if along_x else pl.ds(x * cy + y, 8)

    def shifted(x, y, i, sign, along_x):
        ex, ey, _ = VELOCITIES[i]
        row = (x + 1 - sign * ex) * stride + 8 + y - sign * ey
        return pl.ds(row, 8, stride=stride) if along_x else pl.ds(row, 8)

    def padded(x, y, along_x):
        row = (x + 1) * stride + 8 + y
        return pl.ds(row, 8, stride=stride) if along_x else pl.ds(row, 8)

    def fractions(rows):
        porous_here = porous[rows, :].astype(jnp.float32)
        wall = walls[rows, :] == 1
        phi = jnp.where(wall, 1.0, porous_here * porosity[rows, :])
        return phi, jnp.where(wall, 0.0, porous_here)

    def pack(stage, values, x, y, sign):
        side = 1 if y else -1
        which = 0 if side > 0 else 1
        for k, i in enumerate(Y_GROUP[side * sign]):
            y_send[stage, which, k, pl.ds(x, 8), :] = values[i]
        for number, (sx, sy) in enumerate(CORNERS):
            if sy == side and x == (cx - 8 if sx > 0 else 0):
                value = values[CORNER_POP[(sx * sign, sy * sign)]]
                row = 7 if sx > 0 else 0
                c_send[stage, number, :, :] = value[row : row + 1, :]

    def step_one(x, y, along_x):
        rows = window(x, y, along_x)
        f = [pops[i, rows, :] for i in range(19)]
        phi, _ = fractions(rows)
        values = [spin(v, VELOCITIES[i][2]) for i, v in enumerate(forward(f, phi))]
        if along_x:
            pack(0, values, x, y, 1)
        else:
            for i in range(19):
                ahead[POS[i], padded(x, y, False), :] = values[i]

    def step_two(x, y, along_x):
        rows = window(x, y, along_x)
        f = [ahead[POS[i], shifted(x, y, i, 1, along_x), :] for i in range(19)]
        a = [adj[i, rows, :] for i in range(19)]
        phi, weight = fractions(rows)
        values, sens = backward(f, a, phi)
        values = [spin(v, -VELOCITIES[i][2]) for i, v in enumerate(values)]
        late_sens[rows, :] = weight * sens
        if along_x:
            pack(1, values, x, y, -1)
        for i in range(19):
            behind[POS[i], padded(x, y, along_x), :] = values[i]

    def step_three(x, y, along_x):
        rows = window(x, y, along_x)
        f = [pops[i, rows, :] for i in range(19)]
        a = [behind[POS[i], shifted(x, y, i, -1, along_x), :] for i in range(19)]
        phi, weight = fractions(rows)
        values, sens = backward(f, a, phi)
        early_sens[rows, :] = weight * sens
        for i in range(19):
            out[i, rows, :] = values[i]

    def y_edges(step):
        for y in (0, cy - 1):
            for x in range(0, cx, 8):
                step(x, y, True)

    def x_faces(step):
        for x in (0, cx - 1):
            for y in range(0, cy, 8):
                step(x, y, False)

    def inner(step):
        @pl.loop(1, cx - 1)
        def _(x):
            for y in range(0, cy, 8):
                step(x, y, False)

    def send(stage, number, src, dst, dx, dy):
        copy = pltpu.make_async_remote_copy(
            src_ref=src, dst_ref=dst,
            send_sem=halo_send.at[stage, number], recv_sem=halo_recv.at[stage, number],
            device_id=near(dx, dy), device_id_type=MESH,
        )
        copy.start()
        return copy

    def send_y(stage):
        copies = [
            send(stage, which, y_send.at[stage, which], y_recv.at[stage, which], 0, side)
            for which, side in enumerate((1, -1))
        ]
        for number, (sx, sy) in enumerate(CORNERS):
            copies.append(
                send(stage, 2 + number, c_send.at[stage, number], c_recv.at[stage, number], sx, sy)
            )
        return copies

    def send_x(stage, buffer, sign):
        copies = []
        for which, side in enumerate((1, -1)):
            group = pl.ds(X_START[side * sign], 5)
            source = (cx if side > 0 else 1) * stride + 8
            target = (0 if side > 0 else cx + 1) * stride + 8
            copies.append(send(
                stage, 6 + which, buffer.at[group, pl.ds(source, cy), :],
                buffer.at[group, pl.ds(target, cy), :], side, 0,
            ))
        return copies

    def receive(stage, copies, buffer, sign):
        for copy in copies:
            copy.wait_recv()
        for which, side in enumerate((1, -1)):
            row = 8 + (-1 if side > 0 else cy)
            for k, i in enumerate(Y_GROUP[side * sign]):
                for x in range(0, cx, 8):
                    buffer[POS[i], pl.ds((x + 1) * stride + row, 8, stride=stride), :] = (
                        y_recv[stage, which, k, pl.ds(x, 8), :]
                    )
        for number, (sx, sy) in enumerate(CORNERS):
            i = CORNER_POP[(sx * sign, sy * sign)]
            row = (0 if sx > 0 else cx + 1) * stride + 8 + (-1 if sy > 0 else cy)
            buffer[POS[i], pl.ds(row, 1), :] = c_recv[stage, number]

    for load in loads[:4]:
        load.wait()
    y_edges(step_one)
    pl.semaphore_wait(barrier, n - 1)
    copies = send_y(0)
    x_faces(step_one)
    copies += send_x(0, ahead, 1)
    inner(step_one)
    loads[4].wait()
    inner(step_two)
    receive(0, copies, ahead, 1)
    y_edges(step_two)
    later = send_y(1)
    x_faces(step_two)
    later += send_x(1, behind, -1)
    inner(step_three)
    receive(1, later, behind, -1)
    y_edges(step_three)
    x_faces(step_three)

    store = pltpu.make_async_copy(out, out_hbm, store_sem)
    store.start()

    rows_of = []
    for x in range(0, cx, 2):
        part = None
        for start in (x * cy, x * cy + 1, (x + 1) * cy, (x + 1) * cy + 1):
            for sens in (late_sens, early_sens):
                piece = sens[pl.ds(start, cy // 2, stride=2), :]
                part = piece if part is None else part + piece
        rows_of.append(part)
    blocks = (cx // 2) * (cy // 2)
    rows_of.append(jnp.zeros((nz - blocks, nz), jnp.float32))
    contract = (((1,), (1,)), ((), ()))
    ones = jnp.ones((8, nz), jnp.float32)
    sums = lax.dot_general(
        ones, jnp.concatenate(rows_of, axis=0), contract,
        precision=lax.Precision.HIGHEST, preferred_element_type=jnp.float32,
    )
    note = sums[0:1, :] + ids_ref[...]
    message[0] = note
    gathered[0] = note

    def patch_copy(k):
        return pltpu.make_async_remote_copy(
            src_ref=message.at[0], dst_ref=gathered.at[k],
            send_sem=patch_send, recv_sem=patch_recv,
            device_id=place(k), device_id_type=MESH,
        )

    @pl.loop(1, n)
    def _(k):
        patch_copy(k).start()

    for copy in copies + later:
        copy.wait_send()
    others = gathered.at[pl.ds(1, n - 1)]
    pltpu.make_async_copy(others, others, patch_recv).wait()

    lane = lax.broadcasted_iota(jnp.int32, (1, nz), 1)
    low = lane < nz // 2
    patch = lax.broadcasted_iota(jnp.int32, (PATCH_DEV, nz), 0).astype(jnp.float32)
    base = (me * PATCH_DEV).astype(jnp.float32)

    def add(k, total):
        one, two = gathered[k], gathered[k + n // 2]
        one_turned, two_turned = pltpu.roll(one, nz // 2, 1), pltpu.roll(two, nz // 2, 1)
        values = jnp.where(low, one, two_turned)
        names = jnp.where(low, one_turned, two) - base
        return total + jnp.where(names == patch, values, 0.0)

    total = lax.fori_loop(0, n // 2, add, jnp.zeros((PATCH_DEV, nz), jnp.float32))
    summed = lax.dot_general(
        ones, total, contract,
        precision=lax.Precision.HIGHEST, preferred_element_type=jnp.float32,
    )
    patch_ref[...] = summed[0:1, :]
    pltpu.make_async_copy(others, others, patch_send).wait()
    store.wait()


def body(sizes, populations, porosity, adjoint_in, porous, walls, owners, slots):
    _, cx, cy, nz = populations.shape
    rows = cx * cy
    n = sizes[0] * sizes[1]
    ids = (owners.reshape(1, -1) * PATCH_DEV + slots.reshape(1, -1)).astype(jnp.float32)
    ids = jnp.concatenate([jnp.zeros((1, nz - ids.shape[1]), jnp.float32), ids], axis=1)
    flat = lambda v: v.reshape(v.shape[:-3] + (rows, nz))
    anywhere = pl.BlockSpec(memory_space=pl.ANY)
    vmem = pl.BlockSpec(memory_space=pltpu.VMEM)
    wide = (19, (cx + 2) * (cy + 16), nz)
    f32 = jnp.float32
    result, patch = pl.pallas_call(
        partial(kernel, (*sizes, cx, cy, nz)),
        out_shape=(
            jax.ShapeDtypeStruct((19, rows, nz), f32), jax.ShapeDtypeStruct((1, PATCH_DEV), f32)
        ),
        in_specs=[anywhere] * 5 + [vmem],
        out_specs=(anywhere, vmem),
        scratch_shapes=[
            pltpu.VMEM((19, rows, nz), f32),
            pltpu.VMEM((rows, nz), f32),
            pltpu.VMEM((19, rows, nz), f32),
            pltpu.VMEM((rows, nz), jnp.int32),
            pltpu.VMEM((rows, nz), jnp.int32),
            pltpu.VMEM((19, rows, nz), f32),
            pltpu.VMEM(wide, f32),
            pltpu.VMEM(wide, f32),
            pltpu.VMEM((rows, nz), f32),
            pltpu.VMEM((rows, nz), f32),
            pltpu.VMEM((2, 2, 5, cx, nz), f32),
            pltpu.VMEM((2, 2, 5, cx, nz), f32),
            pltpu.VMEM((2, 4, 1, nz), f32),
            pltpu.VMEM((2, 4, 1, nz), f32),
            pltpu.VMEM((1, 1, nz), f32),
            pltpu.VMEM((n, 1, nz), f32),
            pltpu.SemaphoreType.DMA((5,)),
            pltpu.SemaphoreType.DMA,
            pltpu.SemaphoreType.DMA((2, 8)),
            pltpu.SemaphoreType.DMA((2, 8)),
            pltpu.SemaphoreType.DMA,
            pltpu.SemaphoreType.DMA,
        ],
        compiler_params=pltpu.CompilerParams(
            collective_id=0, has_side_effects=True, vmem_limit_bytes=40 * 1024 * 1024
        ),
    )(flat(populations), flat(porosity), flat(adjoint_in), flat(porous), flat(walls), ids)
    return result.reshape(populations.shape), patch.reshape(-1)


def solution(mesh):
    sizes = (mesh.shape["gx"], mesh.shape["gy"])
    return jax.shard_map(
        partial(body, sizes),
        mesh=mesh,
        in_specs=(
            P(None, "gx", "gy", None),
            P("gx", "gy", None),
            P(None, "gx", "gy", None),
            P("gx", "gy", None),
            P("gx", "gy", None),
            P("gx", "gy", None, None),
            P("gx", "gy", None),
        ),
        out_specs=(P(None, "gx", "gy", None), P(("gx", "gy"))),
        check_vma=False,
    )
```

```python
from functools import partial

import jax
import jax.numpy as jnp
from jax import lax
from jax.experimental import pallas as pl
from jax.experimental.pallas import tpu as pltpu
from jax.sharding import PartitionSpec as P

PATCH_DEV = 256
MESH = pl.DeviceIdType.MESH

VELOCITIES = [
    (0, 0, 0),
    (1, 0, 0), (-1, 0, 0), (0, 1, 0), (0, -1, 0), (0, 0, 1), (0, 0, -1),
    (1, 1, 0), (-1, -1, 0), (1, -1, 0), (-1, 1, 0),
    (1, 0, 1), (-1, 0, -1), (1, 0, -1), (-1, 0, 1),
    (0, 1, 1), (0, -1, -1), (0, 1, -1), (0, -1, 1),
]
ORDER = [0, 3, 4, 5, 6, 15, 16, 17, 18, 1, 7, 9, 11, 13, 2, 8, 10, 12, 14]
POS = [ORDER.index(i) for i in range(19)]
X_START = {1: 9, -1: 14}
Y_GROUP = {1: [3, 7, 10, 15, 17], -1: [4, 8, 9, 16, 18]}
CORNERS = [(1, 1), (-1, -1), (1, -1), (-1, 1)]
CORNER_POP = {(1, 1): 7, (-1, -1): 8, (1, -1): 9, (-1, 1): 10}
PLANES = (7, 11, 15)
RATE2, RATE3, RATE4 = 1.25, 1.5, 1.4


def split_planes(f):
    out = []
    for start in PLANES:
        a, b, c, d = f[start : start + 4]
        s1, s2, t1, t2 = a + b, c + d, a - b, c - d
        out.append((s1 + s2, s1 - s2, t1 + t2, t1 - t2, t1, t2))
    return out


def split_faces(f):
    return [f[1] + f[2], f[3] + f[4], f[5] + f[6]], [f[1] - f[2], f[3] - f[4], f[5] - f[6]]


def nonequilibrium(f):
    (w_xy, w_xz, w_yz) = planes = split_planes(f)
    sums, diffs = split_faces(f)
    second = [sums[0] + w_xy[0] + w_xz[0], sums[1] + w_xy[0] + w_yz[0], sums[2] + w_xz[0] + w_yz[0]]
    jx = diffs[0] + (w_xy[2] + w_xz[2])
    jy = diffs[1] + (w_xy[3] + w_yz[2])
    jz = diffs[2] + (w_xz[3] + w_yz[3])
    rho = (f[0] + sums[0]) + (sums[1] + sums[2]) + ((w_xy[0] + w_xz[0]) + w_yz[0])
    inverse = 1.0 / rho
    ux, uy, uz = jx * inverse, jy * inverse, jz * inverse
    qx, qy, qz = jx * ux, jy * uy, jz * uz
    third_rho = rho * (1.0 / 3.0)
    second = [second[0] - third_rho - qx, second[1] - third_rho - qy, second[2] - third_rho - qz]
    product = [w_xy[1] - jx * uy, w_xz[1] - jx * uz, w_yz[1] - jy * uz]
    kx, ky, kz = jx * (1.0 / 3.0), jy * (1.0 / 3.0), jz * (1.0 / 3.0)
    first = [w_xy[2] - kx, w_xz[2] - kx, w_yz[2] - ky]
    other = [w_xy[3] - ky, w_xz[3] - kz, w_yz[3] - kz]
    base = rho * (1.0 / 9.0) + ((qx + qy) + qz) * (1.0 / 3.0)
    fourth = [w_xy[0] - base + 0.5 * qz, w_xz[0] - base + 0.5 * qy, w_yz[0] - base + 0.5 * qx]
    return planes, diffs, (ux, uy, uz), (second, product, first, other, fourth)


def forward(f, phi):
    _, _, u, (second, product, first, other, fourth) = nonequilibrium(f)
    second = [v * (0.5 * RATE2) for v in second]
    product = [v * (0.25 * RATE2) for v in product]
    first = [v * (0.25 * RATE3) for v in first]
    other = [v * (0.25 * RATE3) for v in other]
    fourth = [v * (0.25 * RATE4) for v in fourth]
    change = [None] * 19
    change[0] = 4.0 * (fourth[0] + fourth[1] + fourth[2]) - 2.0 * (second[0] + second[1] + second[2])
    evens = [
        second[0] - 2.0 * (fourth[0] + fourth[1]),
        second[1] - 2.0 * (fourth[0] + fourth[2]),
        second[2] - 2.0 * (fourth[1] + fourth[2]),
    ]
    odds = [
        2.0 * (first[0] + first[1]),
        2.0 * (other[0] + first[2]),
        2.0 * (other[1] + other[2]),
    ]
    for axis in range(3):
        change[1 + 2 * axis] = evens[axis] - odds[axis]
        change[2 + 2 * axis] = evens[axis] + odds[axis]
    for plane, start in enumerate(PLANES):
        h, k = fourth[plane] + product[plane], fourth[plane] - product[plane]
        p, q = first[plane] + other[plane], first[plane] - other[plane]
        change[start : start + 4] = [h + p, h - p, k + q, k - q]
    relaxed = [f[i] - change[i] for i in range(19)]
    opposite = [0] + [i + 1 if i % 2 else i - 1 for i in range(1, 19)]
    gap = [f[opposite[i]] - relaxed[i] for i in range(19)]
    return [relaxed[i] + phi * gap[i] for i in range(19)], gap, u


def adjoint_moments(a):
    a_planes = split_planes(a)
    a_sums, a_diffs = split_faces(a)
    half = [0.5 * v for v in a_sums]
    n_xy, n_xz, n_yz = a_planes
    b2 = [RATE2 * (v - a[0]) for v in half]
    b11 = [(0.25 * RATE2) * n[1] for n in a_planes]
    hx, hy, hz = [(0.5 * RATE3) * v for v in a_diffs]
    b_first = [
        (0.25 * RATE3) * n_xy[2] - hx, (0.25 * RATE3) * n_xz[2] - hx, (0.25 * RATE3) * n_yz[2] - hy
    ]
    b_other = [
        (0.25 * RATE3) * n_xy[3] - hy, (0.25 * RATE3) * n_xz[3] - hz, (0.25 * RATE3) * n_yz[3] - hz
    ]
    b4 = [
        RATE4 * (0.25 * n_xy[0] - (half[0] + half[1]) + a[0]),
        RATE4 * (0.25 * n_xz[0] - (half[0] + half[2]) + a[0]),
        RATE4 * (0.25 * n_yz[0] - (half[1] + half[2]) + a[0]),
    ]
    return a_planes, a_diffs, (b2, b11, b_first, b_other, b4)


def fraction_cotangent(f_planes, f_diffs, moments, a_planes, a_diffs, b):
    parts = []
    for mine, theirs in zip(b, moments):
        part = None
        for v, m in zip(mine, theirs):
            part = v * m if part is None else part + v * m
        parts.append(part)
    for axis in range(3):
        parts[axis] = parts[axis] - f_diffs[axis] * a_diffs[axis]
    for k, (p, n) in enumerate(zip(f_planes, a_planes)):
        parts[k + 2] = parts[k + 2] - p[4] * n[4] - p[5] * n[5]
    return ((parts[0] + parts[1]) + (parts[2] + parts[3])) + parts[4]


def population_cotangent(u, a, b, phi):
    ux, uy, uz = u
    b2, b11, b_first, b_other, b4 = b
    keep = 1.0 - phi
    b2, b11, b_first, b_other, b4 = [
        [keep * v for v in part] for part in (b2, b11, b_first, b_other, b4)
    ]
    total4 = b4[0] + b4[1] + b4[2]
    twice = total4 * (2.0 / 3.0)
    cx, cy, cz = 2.0 * b2[0] + twice - b4[2], 2.0 * b2[1] + twice - b4[1], 2.0 * b2[2] + twice - b4[0]
    wx = cx * ux + b11[0] * uy + b11[1] * uz
    wy = cy * uy + b11[0] * ux + b11[2] * uz
    wz = cz * uz + b11[1] * ux + b11[2] * uy
    r0 = (
        0.5 * (ux * wx + uy * wy + uz * wz)
        - (b2[0] + b2[1] + b2[2]) * (1.0 / 3.0)
        - total4 * (1.0 / 9.0)
    )
    rx = -(b_first[0] + b_first[1]) * (1.0 / 3.0) - wx
    ry = -(b_other[0] + b_first[2]) * (1.0 / 3.0) - wy
    rz = -(b_other[1] + b_other[2]) * (1.0 / 3.0) - wz
    result = [None] * 19
    result[0] = a[0] - r0
    evens = [r0 + b2[0], r0 + b2[1], r0 + b2[2]]
    for axis, odd in enumerate((rx, ry, rz)):
        back = phi * (a[1 + 2 * axis] - a[2 + 2 * axis]) + odd
        result[1 + 2 * axis] = (a[1 + 2 * axis] - evens[axis]) - back
        result[2 + 2 * axis] = (a[2 + 2 * axis] - evens[axis]) + back
    for plane, (start, one, two) in enumerate(((7, 0, 1), (11, 0, 2), (15, 1, 2))):
        even = evens[one] + b2[two] + b4[plane]
        p = (rx, ry, rz)[one] + b_first[plane]
        q = (rx, ry, rz)[two] + b_other[plane]
        h, k = even + b11[plane], even - b11[plane]
        s = (p + q) + phi * (a[start] - a[start + 1])
        t = (p - q) + phi * (a[start + 2] - a[start + 3])
        result[start] = (a[start] - h) - s
        result[start + 1] = (a[start + 1] - h) + s
        result[start + 2] = (a[start + 2] - k) - t
        result[start + 3] = (a[start + 3] - k) + t
    return result


def kernel(
    sizes, pops_hbm, porosity_hbm, adj_hbm, porous_hbm, walls_hbm, owners_hbm, slots_hbm,
    out, gathered,
    pops, porosity, adj, porous, walls, owners, slots, gap, speed, ahead, behind,
    late_sens, early_sens, y_send, y_recv, c_send, c_recv, message, names,
    load_sem, halo_send, halo_recv, patch_send, patch_recv,
):
    n_gx, n_gy, cx, cy, nz = sizes
    n = n_gx * n_gy
    stride = cy + 16
    gx, gy = lax.axis_index("gx"), lax.axis_index("gy")
    me = gx * n_gy + gy

    faces = [pl.ds(0, cy), pl.ds((cx - 1) * cy, cy)]
    middle = pl.ds(cy, (cx - 2) * cy)
    pairs = [(porosity_hbm, porosity), (porous_hbm, porous), (walls_hbm, walls)]
    pairs += [(pops_hbm.at[:, part, :], pops.at[:, part, :]) for part in faces + [middle]]
    pairs += [(adj_hbm, adj), (owners_hbm, owners), (slots_hbm, slots)]
    loads = [
        pltpu.make_async_copy(src, dst, load_sem.at[k]) for k, (src, dst) in enumerate(pairs)
    ]
    for load in loads:
        load.start()

    def place(k):
        index = lax.rem(me + k, n)
        return (index // n_gy, lax.rem(index, n_gy))

    barrier = pltpu.get_barrier_semaphore()

    @pl.loop(1, n)
    def _(k):
        pl.semaphore_signal(barrier, inc=1, device_id=place(k), device_id_type=MESH)

    def near(dx, dy):
        return (lax.rem(gx + (dx + n_gx), n_gx), lax.rem(gy + (dy + n_gy), n_gy))

    def spin(value, shift):
        return value if shift == 0 else pltpu.roll(value, shift % nz, 1)

    def window(x, y, along_x):
        return pl.ds(x * cy + y, 8, stride=cy) if along_x else pl.ds(x * cy + y, 8)

    def shifted(x, y, i, sign, along_x):
        ex, ey, _ = VELOCITIES[i]
        row = (x + 1 - sign * ex) * stride + 8 + y - sign * ey
        return pl.ds(row, 8, stride=stride) if along_x else pl.ds(row, 8)

    def padded(x, y, along_x):
        row = (x + 1) * stride + 8 + y
        return pl.ds(row, 8, stride=stride) if along_x else pl.ds(row, 8)

    def fractions(rows):
        porous_here = porous[rows, :].astype(jnp.float32)
        wall = walls[rows, :] == 1
        phi = jnp.where(wall, 1.0, porous_here * porosity[rows, :])
        return phi, jnp.where(wall, 0.0, porous_here)

    def pack(stage, values, x, y, sign):
        side = 1 if y else -1
        which = 0 if side > 0 else 1
        for k, i in enumerate(Y_GROUP[side * sign]):
            y_send[stage, which, k, pl.ds(x, 8), :] = values[i]
        for number, (sx, sy) in enumerate(CORNERS):
            if sy == side and x == (cx - 8 if sx > 0 else 0):
                value = values[CORNER_POP[(sx * sign, sy * sign)]]
                row = 7 if sx > 0 else 0
                c_send[stage, number, :, :] = value[row : row + 1, :]

    def step_one(x, y, along_x):
        rows = window(x, y, along_x)
        f = [pops[i, rows, :] for i in range(19)]
        phi, _ = fractions(rows)
        values, apart, u = forward(f, phi)
        values = [spin(v, VELOCITIES[i][2]) for i, v in enumerate(values)]
        if along_x:
            pack(0, values, x, y, 1)
        else:
            for i in range(19):
                ahead[POS[i], padded(x, y, False), :] = values[i]
                gap[i, rows, :] = apart[i]
            for axis in range(3):
                speed[axis, rows, :] = u[axis]

    def step_two(x, y, along_x):
        rows = window(x, y, along_x)
        f = [ahead[POS[i], shifted(x, y, i, 1, along_x), :] for i in range(19)]
        phi, weight = fractions(rows)
        f_planes, f_diffs, u, moments = nonequilibrium(f)
        a_planes, a_diffs, b = adjoint_moments([adj[i, rows, :] for i in range(19)])
        sens = fraction_cotangent(f_planes, f_diffs, moments, a_planes, a_diffs, b)
        late_sens[rows, :] = weight * sens
        values = population_cotangent(u, [adj[i, rows, :] for i in range(19)], b, phi)
        values = [spin(v, -VELOCITIES[i][2]) for i, v in enumerate(values)]
        if along_x:
            pack(1, values, x, y, -1)
        for i in range(19):
            behind[POS[i], padded(x, y, along_x), :] = values[i]

    def pulled(x, y, along_x):
        return [behind[POS[i], shifted(x, y, i, -1, along_x), :] for i in range(19)]

    def step_sens(x, y, along_x):
        rows = window(x, y, along_x)
        a = pulled(x, y, along_x)
        parts = [a[i] * gap[i, rows, :] for i in range(4)]
        for i in range(4, 19):
            parts[i % 4] = parts[i % 4] + a[i] * gap[i, rows, :]
        _, weight = fractions(rows)
        early_sens[rows, :] = weight * ((parts[0] + parts[1]) + (parts[2] + parts[3]))

    def step_out(x, y, along_x):
        rows = window(x, y, along_x)
        phi, _ = fractions(rows)
        _, _, b = adjoint_moments(pulled(x, y, along_x))
        u = [speed[axis, rows, :] for axis in range(3)]
        values = population_cotangent(u, pulled(x, y, along_x), b, phi)
        for i in range(19):
            out[i, rows, :] = values[i]

    def step_three(x, y, along_x):
        step_sens(x, y, along_x)
        step_out(x, y, along_x)

    def y_edges(step):
        for y in (0, cy - 1):
            for x in range(0, cx, 8):
                step(x, y, True)

    def x_faces(step):
        for x in (0, cx - 1):
            for y in range(0, cy, 8):
                step(x, y, False)

    def inner(step, start, stop):
        @pl.loop(start, stop)
        def _(x):
            for y in range(0, cy, 8):
                step(x, y, False)

    def send(stage, number, src, dst, dx, dy):
        copy = pltpu.make_async_remote_copy(
            src_ref=src, dst_ref=dst,
            send_sem=halo_send.at[stage, number], recv_sem=halo_recv.at[stage, number],
            device_id=near(dx, dy), device_id_type=MESH,
        )
        copy.start()
        return copy

    def send_y(stage):
        copies = [
            send(stage, which, y_send.at[stage, which], y_recv.at[stage, which], 0, side)
            for which, side in enumerate((1, -1))
        ]
        for number, (sx, sy) in enumerate(CORNERS):
            copies.append(
                send(stage, 2 + number, c_send.at[stage, number], c_recv.at[stage, number], sx, sy)
            )
        return copies

    def send_x(stage, buffer, sign):
        copies = []
        for which, side in enumerate((1, -1)):
            group = pl.ds(X_START[side * sign], 5)
            source = (cx if side > 0 else 1) * stride + 8
            target = (0 if side > 0 else cx + 1) * stride + 8
            copies.append(send(
                stage, 6 + which, buffer.at[group, pl.ds(source, cy), :],
                buffer.at[group, pl.ds(target, cy), :], side, 0,
            ))
        return copies

    def receive(stage, copies, buffer, sign):
        for copy in copies:
            copy.wait_recv()
        for which, side in enumerate((1, -1)):
            row = 8 + (-1 if side > 0 else cy)
            for k, i in enumerate(Y_GROUP[side * sign]):
                for x in range(0, cx, 8):
                    buffer[POS[i], pl.ds((x + 1) * stride + row, 8, stride=stride), :] = (
                        y_recv[stage, which, k, pl.ds(x, 8), :]
                    )
        for number, (sx, sy) in enumerate(CORNERS):
            i = CORNER_POP[(sx * sign, sy * sign)]
            row = (0 if sx > 0 else cx + 1) * stride + 8 + (-1 if sy > 0 else cy)
            buffer[POS[i], pl.ds(row, 1), :] = c_recv[stage, number]

    names[...] = jnp.zeros_like(names)
    for load in loads[:5]:
        load.wait()
    x_faces(step_one)
    pl.semaphore_wait(barrier, n - 1)
    copies = send_x(0, ahead, 1)
    loads[5].wait()
    y_edges(step_one)
    copies += send_y(0)
    inner(step_one, 1, cx - 1)
    for load in loads[6:]:
        load.wait()
    names[pl.ds(0, 1), pl.ds(0, owners.shape[1])] = (
        owners[...] * PATCH_DEV + slots[...]
    ).astype(jnp.float32)
    inner(step_two, 1, cx // 2)
    receive(0, copies, ahead, 1)
    y_edges(step_two)
    later = send_y(1)
    x_faces(step_two)
    later += send_x(1, behind, -1)
    inner(step_two, cx // 2, cx - 1)
    inner(step_three, 1, cx - 1)
    receive(1, later, behind, -1)
    y_edges(step_sens)
    x_faces(step_sens)

    rows_of = []
    for x in range(0, cx, 2):
        part = None
        for start in (x * cy, x * cy + 1, (x + 1) * cy, (x + 1) * cy + 1):
            for sens in (late_sens, early_sens):
                piece = sens[pl.ds(start, cy // 2, stride=2), :]
                part = piece if part is None else part + piece
        rows_of.append(part)
    blocks = (cx // 2) * (cy // 2)
    rows_of.append(jnp.zeros((nz - blocks, nz), jnp.float32))
    contract = (((1,), (1,)), ((), ()))
    ones = jnp.ones((8, nz), jnp.float32)
    sums = lax.dot_general(
        ones, jnp.concatenate(rows_of, axis=0), contract,
        precision=lax.Precision.HIGHEST, preferred_element_type=jnp.float32,
    )
    note = sums[0:1, :] + pltpu.roll(names[...], nz // 2, 1)[0:1, :]
    message[0] = note
    gathered[0] = note

    def patch_copy(k):
        return pltpu.make_async_remote_copy(
            src_ref=message.at[0], dst_ref=gathered.at[k],
            send_sem=patch_send, recv_sem=patch_recv,
            device_id=place(k), device_id_type=MESH,
        )

    @pl.loop(1, n)
    def _(k):
        patch_copy(k).start()

    y_edges(step_out)
    x_faces(step_out)

    for copy in copies + later:
        copy.wait_send()
    others = gathered.at[pl.ds(1, n - 1)]
    pltpu.make_async_copy(others, others, patch_recv).wait()
    pltpu.make_async_copy(others, others, patch_send).wait()


def finish(sizes, result, gathered, out_hbm, patch_ref, store_sem):
    n_gx, n_gy, _, _, nz = sizes
    n = n_gx * n_gy
    store = pltpu.make_async_copy(result, out_hbm, store_sem)
    store.start()
    me = lax.axis_index("gx") * n_gy + lax.axis_index("gy")
    lane = lax.broadcasted_iota(jnp.int32, (1, nz), 1)
    low = lane < nz // 2
    patch = lax.broadcasted_iota(jnp.int32, (PATCH_DEV, nz), 0).astype(jnp.float32)
    base = (me * PATCH_DEV).astype(jnp.float32)

    def add(k, total):
        one, two = gathered[k], gathered[k + n // 2]
        one_turned, two_turned = pltpu.roll(one, nz // 2, 1), pltpu.roll(two, nz // 2, 1)
        values = jnp.where(low, one, two_turned)
        names = jnp.where(low, one_turned, two) - base
        return total + jnp.where(names == patch, values, 0.0)

    total = lax.fori_loop(0, n // 2, add, jnp.zeros((PATCH_DEV, nz), jnp.float32))
    summed = lax.dot_general(
        jnp.ones((8, nz), jnp.float32), total, (((1,), (1,)), ((), ())),
        precision=lax.Precision.HIGHEST, preferred_element_type=jnp.float32,
    )
    patch_ref[...] = summed[0:1, :]
    store.wait()


def body(sizes, populations, porosity, adjoint_in, porous, walls, owners, slots):
    _, cx, cy, nz = populations.shape
    rows = cx * cy
    n = sizes[0] * sizes[1]
    flat = lambda v: v.reshape(v.shape[:-3] + (rows, nz))
    row = lambda v: v.reshape(1, -1)
    hbm = pl.BlockSpec(memory_space=pltpu.HBM)
    vmem = pl.BlockSpec(memory_space=pltpu.VMEM)
    wide = (19, (cx + 2) * (cy + 16), nz)
    f32 = jnp.float32
    whole = jax.ShapeDtypeStruct((19, rows, nz), f32)
    shape = (*sizes, cx, cy, nz)
    blocks = slots.shape[-1]
    result, gathered = pl.pallas_call(
        partial(kernel, shape),
        out_shape=(whole, jax.ShapeDtypeStruct((n, 1, nz), f32)),
        in_specs=[hbm] * 7,
        out_specs=(vmem, vmem),
        scratch_shapes=[
            pltpu.VMEM((19, rows, nz), f32),
            pltpu.VMEM((rows, nz), f32),
            pltpu.VMEM((19, rows, nz), f32),
            pltpu.VMEM((rows, nz), jnp.int32),
            pltpu.VMEM((rows, nz), jnp.int32),
            pltpu.VMEM((1, blocks), jnp.int32),
            pltpu.VMEM((1, blocks), jnp.int32),
            pltpu.VMEM((19, rows, nz), f32),
            pltpu.VMEM((3, rows, nz), f32),
            pltpu.VMEM(wide, f32),
            pltpu.VMEM(wide, f32),
            pltpu.VMEM((rows, nz), f32),
            pltpu.VMEM((rows, nz), f32),
            pltpu.VMEM((2, 2, 5, cx, nz), f32),
            pltpu.VMEM((2, 2, 5, cx, nz), f32),
            pltpu.VMEM((2, 4, 1, nz), f32),
            pltpu.VMEM((2, 4, 1, nz), f32),
            pltpu.VMEM((1, 1, nz), f32),
            pltpu.VMEM((8, nz), f32),
            pltpu.SemaphoreType.DMA((9,)),
            pltpu.SemaphoreType.DMA((2, 8)),
            pltpu.SemaphoreType.DMA((2, 8)),
            pltpu.SemaphoreType.DMA,
            pltpu.SemaphoreType.DMA,
        ],
        compiler_params=pltpu.CompilerParams(
            collective_id=0, has_side_effects=True, vmem_limit_bytes=40 * 1024 * 1024
        ),
    )(
        *[pltpu.with_memory_space_constraint(v, pltpu.HBM) for v in (flat(populations), flat(porosity), flat(adjoint_in), flat(porous), flat(walls),
        row(owners), row(slots))],
    )
    adjoint_out, patch = pl.pallas_call(
        partial(finish, shape),
        out_shape=(whole, jax.ShapeDtypeStruct((1, PATCH_DEV), f32)),
        in_specs=[vmem, vmem],
        out_specs=(hbm, vmem),
        scratch_shapes=[pltpu.SemaphoreType.DMA],
        compiler_params=pltpu.CompilerParams(vmem_limit_bytes=16 * 1024 * 1024),
    )(result, gathered)
    return adjoint_out.reshape(populations.shape), patch.reshape(-1)


def solution(mesh):
    sizes = (mesh.shape["gx"], mesh.shape["gy"])
    return jax.shard_map(
        partial(body, sizes),
        mesh=mesh,
        in_specs=(
            P(None, "gx", "gy", None),
            P("gx", "gy", None),
            P(None, "gx", "gy", None),
            P("gx", "gy", None),
            P("gx", "gy", None),
            P("gx", "gy", None, None),
            P("gx", "gy", None),
        ),
        out_specs=(P(None, "gx", "gy", None), P(("gx", "gy"))),
        check_vma=False,
    )
```

```python
from collections import namedtuple
from functools import partial

import jax
import jax.numpy as jnp
from jax import lax
from jax.experimental import pallas as pl
from jax.experimental.pallas import tpu as pltpu
from jax.sharding import PartitionSpec as P

PATCH_DEV = 256
MESH = pl.DeviceIdType.MESH

VELOCITIES = [
    (0, 0, 0),
    (1, 0, 0), (-1, 0, 0), (0, 1, 0), (0, -1, 0), (0, 0, 1), (0, 0, -1),
    (1, 1, 0), (-1, -1, 0), (1, -1, 0), (-1, 1, 0),
    (1, 0, 1), (-1, 0, -1), (1, 0, -1), (-1, 0, 1),
    (0, 1, 1), (0, -1, -1), (0, 1, -1), (0, -1, 1),
]
ORDER = [0, 3, 4, 5, 6, 15, 16, 17, 18, 1, 7, 9, 11, 13, 2, 8, 10, 12, 14]
POS = [ORDER.index(i) for i in range(19)]
X_START = {1: 9, -1: 14}
Y_GROUP = {1: [3, 7, 10, 15, 17], -1: [4, 8, 9, 16, 18]}
CORNERS = [(1, 1), (-1, -1), (1, -1), (-1, 1)]
CORNER_POP = {(1, 1): 7, (-1, -1): 8, (1, -1): 9, (-1, 1): 10}
PLANES = (7, 11, 15)
RATE2, RATE3, RATE4 = 1.25, 1.5, 1.4


Node = namedtuple("Node", [
    "pops", "porosity", "adj", "porous", "walls", "out", "gap", "speed", "late_sens", "early_sens",
    "ahead", "behind",
])


def split_planes(f):
    out = []
    for start in PLANES:
        a, b, c, d = f[start : start + 4]
        s1, s2, t1, t2 = a + b, c + d, a - b, c - d
        out.append((s1 + s2, s1 - s2, t1 + t2, t1 - t2, t1, t2))
    return out


def split_faces(f):
    return [f[1] + f[2], f[3] + f[4], f[5] + f[6]], [f[1] - f[2], f[3] - f[4], f[5] - f[6]]


def nonequilibrium(f):
    (w_xy, w_xz, w_yz) = planes = split_planes(f)
    sums, diffs = split_faces(f)
    second = [sums[0] + w_xy[0] + w_xz[0], sums[1] + w_xy[0] + w_yz[0], sums[2] + w_xz[0] + w_yz[0]]
    jx = diffs[0] + (w_xy[2] + w_xz[2])
    jy = diffs[1] + (w_xy[3] + w_yz[2])
    jz = diffs[2] + (w_xz[3] + w_yz[3])
    rho = (f[0] + sums[0]) + (sums[1] + sums[2]) + ((w_xy[0] + w_xz[0]) + w_yz[0])
    inverse = 1.0 / rho
    ux, uy, uz = jx * inverse, jy * inverse, jz * inverse
    qx, qy, qz = jx * ux, jy * uy, jz * uz
    third_rho = rho * (1.0 / 3.0)
    second = [second[0] - third_rho - qx, second[1] - third_rho - qy, second[2] - third_rho - qz]
    product = [w_xy[1] - jx * uy, w_xz[1] - jx * uz, w_yz[1] - jy * uz]
    kx, ky, kz = jx * (1.0 / 3.0), jy * (1.0 / 3.0), jz * (1.0 / 3.0)
    first = [w_xy[2] - kx, w_xz[2] - kx, w_yz[2] - ky]
    other = [w_xy[3] - ky, w_xz[3] - kz, w_yz[3] - kz]
    base = rho * (1.0 / 9.0) + ((qx + qy) + qz) * (1.0 / 3.0)
    fourth = [w_xy[0] - base + 0.5 * qz, w_xz[0] - base + 0.5 * qy, w_yz[0] - base + 0.5 * qx]
    return planes, diffs, (ux, uy, uz), (second, product, first, other, fourth)


def forward(f, phi):
    _, _, u, (second, product, first, other, fourth) = nonequilibrium(f)
    second = [v * (0.5 * RATE2) for v in second]
    product = [v * (0.25 * RATE2) for v in product]
    first = [v * (0.25 * RATE3) for v in first]
    other = [v * (0.25 * RATE3) for v in other]
    fourth = [v * (0.25 * RATE4) for v in fourth]
    change = [None] * 19
    change[0] = 4.0 * (fourth[0] + fourth[1] + fourth[2]) - 2.0 * (second[0] + second[1] + second[2])
    evens = [
        second[0] - 2.0 * (fourth[0] + fourth[1]),
        second[1] - 2.0 * (fourth[0] + fourth[2]),
        second[2] - 2.0 * (fourth[1] + fourth[2]),
    ]
    odds = [
        2.0 * (first[0] + first[1]),
        2.0 * (other[0] + first[2]),
        2.0 * (other[1] + other[2]),
    ]
    for axis in range(3):
        change[1 + 2 * axis] = evens[axis] - odds[axis]
        change[2 + 2 * axis] = evens[axis] + odds[axis]
    for plane, start in enumerate(PLANES):
        h, k = fourth[plane] + product[plane], fourth[plane] - product[plane]
        p, q = first[plane] + other[plane], first[plane] - other[plane]
        change[start : start + 4] = [h + p, h - p, k + q, k - q]
    relaxed = [f[i] - change[i] for i in range(19)]
    opposite = [0] + [i + 1 if i % 2 else i - 1 for i in range(1, 19)]
    gap = [f[opposite[i]] - relaxed[i] for i in range(19)]
    return [relaxed[i] + phi * gap[i] for i in range(19)], gap, u


def adjoint_moments(a):
    a_planes = split_planes(a)
    a_sums, a_diffs = split_faces(a)
    half = [0.5 * v for v in a_sums]
    n_xy, n_xz, n_yz = a_planes
    b2 = [RATE2 * (v - a[0]) for v in half]
    b11 = [(0.25 * RATE2) * n[1] for n in a_planes]
    hx, hy, hz = [(0.5 * RATE3) * v for v in a_diffs]
    b_first = [
        (0.25 * RATE3) * n_xy[2] - hx, (0.25 * RATE3) * n_xz[2] - hx, (0.25 * RATE3) * n_yz[2] - hy
    ]
    b_other = [
        (0.25 * RATE3) * n_xy[3] - hy, (0.25 * RATE3) * n_xz[3] - hz, (0.25 * RATE3) * n_yz[3] - hz
    ]
    b4 = [
        RATE4 * (0.25 * n_xy[0] - (half[0] + half[1]) + a[0]),
        RATE4 * (0.25 * n_xz[0] - (half[0] + half[2]) + a[0]),
        RATE4 * (0.25 * n_yz[0] - (half[1] + half[2]) + a[0]),
    ]
    return a_planes, a_diffs, (b2, b11, b_first, b_other, b4)


def fraction_cotangent(f_planes, f_diffs, moments, a_planes, a_diffs, b):
    parts = []
    for mine, theirs in zip(b, moments):
        part = None
        for v, m in zip(mine, theirs):
            part = v * m if part is None else part + v * m
        parts.append(part)
    for axis in range(3):
        parts[axis] = parts[axis] - f_diffs[axis] * a_diffs[axis]
    for k, (p, n) in enumerate(zip(f_planes, a_planes)):
        parts[k + 2] = parts[k + 2] - p[4] * n[4] - p[5] * n[5]
    return ((parts[0] + parts[1]) + (parts[2] + parts[3])) + parts[4]


def population_cotangent(u, a, b, phi):
    ux, uy, uz = u
    b2, b11, b_first, b_other, b4 = b
    keep = 1.0 - phi
    b2, b11, b_first, b_other, b4 = [
        [keep * v for v in part] for part in (b2, b11, b_first, b_other, b4)
    ]
    total4 = b4[0] + b4[1] + b4[2]
    twice = total4 * (2.0 / 3.0)
    cx, cy, cz = 2.0 * b2[0] + twice - b4[2], 2.0 * b2[1] + twice - b4[1], 2.0 * b2[2] + twice - b4[0]
    wx = cx * ux + b11[0] * uy + b11[1] * uz
    wy = cy * uy + b11[0] * ux + b11[2] * uz
    wz = cz * uz + b11[1] * ux + b11[2] * uy
    r0 = (
        0.5 * (ux * wx + uy * wy + uz * wz)
        - (b2[0] + b2[1] + b2[2]) * (1.0 / 3.0)
        - total4 * (1.0 / 9.0)
    )
    rx = -(b_first[0] + b_first[1]) * (1.0 / 3.0) - wx
    ry = -(b_other[0] + b_first[2]) * (1.0 / 3.0) - wy
    rz = -(b_other[1] + b_other[2]) * (1.0 / 3.0) - wz
    result = [None] * 19
    result[0] = a[0] - r0
    evens = [r0 + b2[0], r0 + b2[1], r0 + b2[2]]
    for axis, odd in enumerate((rx, ry, rz)):
        back = phi * (a[1 + 2 * axis] - a[2 + 2 * axis]) + odd
        result[1 + 2 * axis] = (a[1 + 2 * axis] - evens[axis]) - back
        result[2 + 2 * axis] = (a[2 + 2 * axis] - evens[axis]) + back
    for plane, (start, one, two) in enumerate(((7, 0, 1), (11, 0, 2), (15, 1, 2))):
        even = evens[one] + b2[two] + b4[plane]
        p = (rx, ry, rz)[one] + b_first[plane]
        q = (rx, ry, rz)[two] + b_other[plane]
        h, k = even + b11[plane], even - b11[plane]
        s = (p + q) + phi * (a[start] - a[start + 1])
        t = (p - q) + phi * (a[start + 2] - a[start + 3])
        result[start] = (a[start] - h) - s
        result[start + 1] = (a[start + 1] - h) + s
        result[start + 2] = (a[start + 2] - k) - t
        result[start + 3] = (a[start + 3] - k) + t
    return result


def kernel(
    sizes, pops_hbm, porosity_hbm, adj_hbm, porous_hbm, walls_hbm, owners_hbm, slots_hbm,
    out, gathered,
    pops, porosity, adj, porous, walls, owners, slots, gap, speed, ahead, behind,
    late_sens, early_sens, y_send, y_recv, c_send, c_recv, message, names,
    load_sem, halo_send, halo_recv, patch_send, patch_recv,
):
    n_gx, n_gy, cx, cy, nz = sizes
    n = n_gx * n_gy
    stride = cy + 16
    gx, gy = lax.axis_index("gx"), lax.axis_index("gy")
    me = gx * n_gy + gy

    faces = [pl.ds(0, cy), pl.ds((cx - 1) * cy, cy)]
    middle = pl.ds(cy, (cx - 2) * cy)
    pairs = [(porosity_hbm, porosity), (porous_hbm, porous), (walls_hbm, walls)]
    pairs += [(pops_hbm.at[:, part, :], pops.at[:, part, :]) for part in faces + [middle]]
    pairs += [(adj_hbm, adj), (owners_hbm, owners), (slots_hbm, slots)]
    loads = [
        pltpu.make_async_copy(src, dst, load_sem.at[k]) for k, (src, dst) in enumerate(pairs)
    ]
    for load in loads:
        load.start()

    def place(k):
        index = lax.rem(me + k, n)
        return (index // n_gy, lax.rem(index, n_gy))

    barrier = pltpu.get_barrier_semaphore()

    @pl.loop(1, n)
    def _(k):
        pl.semaphore_signal(barrier, inc=1, device_id=place(k), device_id_type=MESH)

    def near(dx, dy):
        return (lax.rem(gx + (dx + n_gx), n_gx), lax.rem(gy + (dy + n_gy), n_gy))

    def spin(value, shift):
        return value if shift == 0 else pltpu.roll(value, shift % nz, 1)

    def window(x, y, along_x):
        return pl.ds(x * cy + y, 8, stride=cy) if along_x else pl.ds(x * cy + y, 8)

    def shifted(x, y, i, sign, along_x):
        ex, ey, _ = VELOCITIES[i]
        row = (x + 1 - sign * ex) * stride + 8 + y - sign * ey
        return pl.ds(row, 8, stride=stride) if along_x else pl.ds(row, 8)

    def padded(x, y, along_x):
        row = (x + 1) * stride + 8 + y
        return pl.ds(row, 8, stride=stride) if along_x else pl.ds(row, 8)

    whole = Node(
        pops, porosity, adj, porous, walls, out, gap, speed, late_sens, early_sens, ahead, behind
    )

    def layer(x):
        plain = pl.ds(pl.multiple_of(x * cy, cy), cy)
        wide = pl.ds(pl.multiple_of(x * stride, stride), 3 * stride)
        parts = [
            ref.at[plain, :] if len(ref.shape) == 2 else ref.at[:, plain, :] for ref in whole[:10]
        ]
        return Node(*parts, ahead.at[:, wide, :], behind.at[:, wide, :])

    def fractions(node, rows):
        porous_here = node.porous[rows, :].astype(jnp.float32)
        wall = node.walls[rows, :] == 1
        phi = jnp.where(wall, 1.0, porous_here * node.porosity[rows, :])
        return phi, jnp.where(wall, 0.0, porous_here)

    def pack(stage, values, x, y, sign):
        side = 1 if y else -1
        which = 0 if side > 0 else 1
        for k, i in enumerate(Y_GROUP[side * sign]):
            y_send[stage, which, k, pl.ds(x, 8), :] = values[i]
        for number, (sx, sy) in enumerate(CORNERS):
            if sy == side and x == (cx - 8 if sx > 0 else 0):
                value = values[CORNER_POP[(sx * sign, sy * sign)]]
                row = 7 if sx > 0 else 0
                c_send[stage, number, :, :] = value[row : row + 1, :]

    def step_one(node, x, y, along_x):
        rows = window(x, y, along_x)
        f = [node.pops[i, rows, :] for i in range(19)]
        phi, _ = fractions(node, rows)
        values, apart, u = forward(f, phi)
        values = [spin(v, VELOCITIES[i][2]) for i, v in enumerate(values)]
        if along_x:
            pack(0, values, x, y, 1)
        else:
            for i in range(19):
                node.ahead[POS[i], padded(x, y, False), :] = values[i]
                node.gap[i, rows, :] = apart[i]
            for axis in range(3):
                node.speed[axis, rows, :] = u[axis]

    def step_two(node, x, y, along_x):
        rows = window(x, y, along_x)
        f = [node.ahead[POS[i], shifted(x, y, i, 1, along_x), :] for i in range(19)]
        phi, weight = fractions(node, rows)
        f_planes, f_diffs, u, moments = nonequilibrium(f)
        a_planes, a_diffs, b = adjoint_moments([node.adj[i, rows, :] for i in range(19)])
        sens = fraction_cotangent(f_planes, f_diffs, moments, a_planes, a_diffs, b)
        node.late_sens[rows, :] = weight * sens
        values = population_cotangent(u, [node.adj[i, rows, :] for i in range(19)], b, phi)
        values = [spin(v, -VELOCITIES[i][2]) for i, v in enumerate(values)]
        if along_x:
            pack(1, values, x, y, -1)
        for i in range(19):
            node.behind[POS[i], padded(x, y, along_x), :] = values[i]

    def pulled(node, x, y, along_x):
        return [node.behind[POS[i], shifted(x, y, i, -1, along_x), :] for i in range(19)]

    def step_sens(node, x, y, along_x):
        rows = window(x, y, along_x)
        a = pulled(node, x, y, along_x)
        parts = [a[i] * node.gap[i, rows, :] for i in range(4)]
        for i in range(4, 19):
            parts[i % 4] = parts[i % 4] + a[i] * node.gap[i, rows, :]
        _, weight = fractions(node, rows)
        node.early_sens[rows, :] = weight * ((parts[0] + parts[1]) + (parts[2] + parts[3]))

    def step_out(node, x, y, along_x):
        rows = window(x, y, along_x)
        phi, _ = fractions(node, rows)
        _, _, b = adjoint_moments(pulled(node, x, y, along_x))
        u = [node.speed[axis, rows, :] for axis in range(3)]
        values = population_cotangent(u, pulled(node, x, y, along_x), b, phi)
        for i in range(19):
            node.out[i, rows, :] = values[i]

    def y_edges(step, stop):
        for y in (0, cy - 1):
            for x in range(0, stop, 8):
                step(whole, x, y, True)

    def x_faces(step):
        for x in (0, cx - 1):
            for y in range(0, cy, 8):
                step(whole, x, y, False)

    def inner(step, start, stop):
        @pl.loop(start, stop)
        def _(x):
            node = layer(x)
            for y in range(0, cy, 8):
                step(node, 0, y, False)

    def send(stage, number, src, dst, dx, dy):
        copy = pltpu.make_async_remote_copy(
            src_ref=src, dst_ref=dst,
            send_sem=halo_send.at[stage, number], recv_sem=halo_recv.at[stage, number],
            device_id=near(dx, dy), device_id_type=MESH,
        )
        copy.start()
        return copy

    def send_y(stage):
        copies = [
            send(stage, which, y_send.at[stage, which], y_recv.at[stage, which], 0, side)
            for which, side in enumerate((1, -1))
        ]
        for number, (sx, sy) in enumerate(CORNERS):
            copies.append(
                send(stage, 2 + number, c_send.at[stage, number], c_recv.at[stage, number], sx, sy)
            )
        return copies

    def send_x(stage, buffer, sign):
        copies = []
        for which, side in enumerate((1, -1)):
            group = pl.ds(X_START[side * sign], 5)
            source = (cx if side > 0 else 1) * stride + 8
            target = (0 if side > 0 else cx + 1) * stride + 8
            copies.append(send(
                stage, 6 + which, buffer.at[group, pl.ds(source, cy), :],
                buffer.at[group, pl.ds(target, cy), :], side, 0,
            ))
        return copies

    def receive(stage, copies, buffer, sign):
        for copy in copies:
            copy.wait_recv()
        for which, side in enumerate((1, -1)):
            row = 8 + (-1 if side > 0 else cy)
            for k, i in enumerate(Y_GROUP[side * sign]):
                for x in range(0, cx, 8):
                    buffer[POS[i], pl.ds((x + 1) * stride + row, 8, stride=stride), :] = (
                        y_recv[stage, which, k, pl.ds(x, 8), :]
                    )
        for number, (sx, sy) in enumerate(CORNERS):
            i = CORNER_POP[(sx * sign, sy * sign)]
            row = (0 if sx > 0 else cx + 1) * stride + 8 + (-1 if sy > 0 else cy)
            buffer[POS[i], pl.ds(row, 1), :] = c_recv[stage, number]

    names[...] = jnp.zeros_like(names)
    for load in loads[:5]:
        load.wait()
    x_faces(step_one)
    pl.semaphore_wait(barrier, n - 1)
    copies = send_x(0, ahead, 1)
    loads[5].wait()
    y_edges(step_one, cx)
    copies += send_y(0)
    inner(step_one, 1, cx - 1)
    for load in loads[6:]:
        load.wait()
    names[pl.ds(0, 1), pl.ds(0, owners.shape[1])] = (
        owners[...] * PATCH_DEV + slots[...]
    ).astype(jnp.float32)
    inner(step_two, 1, cx // 2)
    receive(0, copies, ahead, 1)
    y_edges(step_two, cx)
    later = send_y(1)
    x_faces(step_two)
    later += send_x(1, behind, -1)
    inner(step_two, cx // 2, cx - 1)
    inner(step_sens, 1, cx - 1)
    inner(step_out, 1, cx // 2)
    receive(1, later, behind, -1)
    y_edges(step_sens, cx)
    x_faces(step_sens)

    rows_of = []
    for x in range(0, cx, 2):
        part = None
        for start in (x * cy, x * cy + 1, (x + 1) * cy, (x + 1) * cy + 1):
            for sens in (late_sens, early_sens):
                piece = sens[pl.ds(start, cy // 2, stride=2), :]
                part = piece if part is None else part + piece
        rows_of.append(part)
    blocks = (cx // 2) * (cy // 2)
    rows_of.append(jnp.zeros((nz - blocks, nz), jnp.float32))
    contract = (((1,), (1,)), ((), ()))
    ones = jnp.ones((8, nz), jnp.float32)
    sums = lax.dot_general(
        ones, jnp.concatenate(rows_of, axis=0), contract,
        precision=lax.Precision.HIGHEST, preferred_element_type=jnp.float32,
    )
    note = sums[0:1, :] + pltpu.roll(names[...], nz // 2, 1)[0:1, :]
    message[0] = note
    gathered[0] = note

    def patch_copy(k):
        return pltpu.make_async_remote_copy(
            src_ref=message.at[0], dst_ref=gathered.at[k],
            send_sem=patch_send, recv_sem=patch_recv,
            device_id=place(k), device_id_type=MESH,
        )

    @pl.loop(1, n)
    def _(k):
        patch_copy(k).start()

    y_edges(step_out, cx // 2)
    x_faces(step_out)
    inner(step_out, cx // 2, cx - 1)

    for copy in copies + later:
        copy.wait_send()
    others = gathered.at[pl.ds(1, n - 1)]
    pltpu.make_async_copy(others, others, patch_recv).wait()
    pltpu.make_async_copy(others, others, patch_send).wait()


def finish(sizes, result, gathered, out_hbm, patch_hbm, patch_ref, store_sem):
    n_gx, n_gy, _, _, nz = sizes
    n = n_gx * n_gy
    parts = [pl.ds(0, 10), pl.ds(10, 9)]
    stores = [
        pltpu.make_async_copy(result.at[part], out_hbm.at[part], store_sem.at[k])
        for k, part in enumerate(parts)
    ]
    for store in stores:
        store.start()
    me = lax.axis_index("gx") * n_gy + lax.axis_index("gy")
    lane = lax.broadcasted_iota(jnp.int32, (1, nz), 1)
    low = lane < nz // 2
    patch = lax.broadcasted_iota(jnp.int32, (PATCH_DEV, nz), 0).astype(jnp.float32)
    base = (me * PATCH_DEV).astype(jnp.float32)

    def add(k, total):
        one, two = gathered[k], gathered[k + n // 2]
        one_turned, two_turned = pltpu.roll(one, nz // 2, 1), pltpu.roll(two, nz // 2, 1)
        values = jnp.where(low, one, two_turned)
        names = jnp.where(low, one_turned, two) - base
        return total + jnp.where(names == patch, values, 0.0)

    total = lax.fori_loop(0, n // 2, add, jnp.zeros((PATCH_DEV, nz), jnp.float32))
    summed = lax.dot_general(
        jnp.ones((8, nz), jnp.float32), total, (((1,), (1,)), ((), ())),
        precision=lax.Precision.HIGHEST, preferred_element_type=jnp.float32,
    )
    patch_ref[...] = summed[0:1, :]
    stores.append(pltpu.make_async_copy(patch_ref, patch_hbm, store_sem.at[2]))
    stores[-1].start()
    for store in stores:
        store.wait()


def body(sizes, populations, porosity, adjoint_in, porous, walls, owners, slots):
    _, cx, cy, nz = populations.shape
    rows = cx * cy
    n = sizes[0] * sizes[1]
    flat = lambda v: v.reshape(v.shape[:-3] + (rows, nz))
    row = lambda v: v.reshape(1, -1)
    hbm = pl.BlockSpec(memory_space=pltpu.HBM)
    vmem = pl.BlockSpec(memory_space=pltpu.VMEM)
    wide = (19, (cx + 2) * (cy + 16), nz)
    f32 = jnp.float32
    whole = jax.ShapeDtypeStruct((19, rows, nz), f32)
    shape = (*sizes, cx, cy, nz)
    blocks = slots.shape[-1]
    arguments = [flat(v) for v in (populations, porosity, adjoint_in, porous, walls)]
    arguments += [row(owners), row(slots)]
    result, gathered = pl.pallas_call(
        partial(kernel, shape),
        out_shape=(whole, jax.ShapeDtypeStruct((n, 1, nz), f32)),
        in_specs=[hbm] * 7,
        out_specs=(vmem, vmem),
        scratch_shapes=[
            pltpu.VMEM((19, rows, nz), f32),
            pltpu.VMEM((rows, nz), f32),
            pltpu.VMEM((19, rows, nz), f32),
            pltpu.VMEM((rows, nz), jnp.int32),
            pltpu.VMEM((rows, nz), jnp.int32),
            pltpu.VMEM((1, blocks), jnp.int32),
            pltpu.VMEM((1, blocks), jnp.int32),
            pltpu.VMEM((19, rows, nz), f32),
            pltpu.VMEM((3, rows, nz), f32),
            pltpu.VMEM(wide, f32),
            pltpu.VMEM(wide, f32),
            pltpu.VMEM((rows, nz), f32),
            pltpu.VMEM((rows, nz), f32),
            pltpu.VMEM((2, 2, 5, cx, nz), f32),
            pltpu.VMEM((2, 2, 5, cx, nz), f32),
            pltpu.VMEM((2, 4, 1, nz), f32),
            pltpu.VMEM((2, 4, 1, nz), f32),
            pltpu.VMEM((1, 1, nz), f32),
            pltpu.VMEM((8, nz), f32),
            pltpu.SemaphoreType.DMA((9,)),
            pltpu.SemaphoreType.DMA((2, 8)),
            pltpu.SemaphoreType.DMA((2, 8)),
            pltpu.SemaphoreType.DMA,
            pltpu.SemaphoreType.DMA,
        ],
        compiler_params=pltpu.CompilerParams(
            collective_id=0, has_side_effects=True, vmem_limit_bytes=40 * 1024 * 1024
        ),
    )(
        *[pltpu.with_memory_space_constraint(v, pltpu.HBM) for v in arguments]
    )
    adjoint_out, patch = pl.pallas_call(
        partial(finish, shape),
        out_shape=(whole, jax.ShapeDtypeStruct((1, PATCH_DEV), f32)),
        in_specs=[vmem, vmem],
        out_specs=(hbm, hbm),
        scratch_shapes=[pltpu.VMEM((1, PATCH_DEV), f32), pltpu.SemaphoreType.DMA((3,))],
        compiler_params=pltpu.CompilerParams(vmem_limit_bytes=16 * 1024 * 1024),
    )(result, gathered)
    return adjoint_out.reshape(populations.shape), patch.reshape(-1)


def solution(mesh):
    sizes = (mesh.shape["gx"], mesh.shape["gy"])
    return jax.shard_map(
        partial(body, sizes),
        mesh=mesh,
        in_specs=(
            P(None, "gx", "gy", None),
            P("gx", "gy", None),
            P(None, "gx", "gy", None),
            P("gx", "gy", None),
            P("gx", "gy", None),
            P("gx", "gy", None, None),
            P("gx", "gy", None),
        ),
        out_specs=(P(None, "gx", "gy", None), P(("gx", "gy"))),
        check_vma=False,
    )
```

```python
from collections import namedtuple
from functools import partial

import jax
import jax.numpy as jnp
from jax import lax
from jax.experimental import pallas as pl
from jax.experimental.pallas import tpu as pltpu
from jax.sharding import PartitionSpec as P

PATCH_DEV = 256
MESH = pl.DeviceIdType.MESH

VELOCITIES = [
    (0, 0, 0),
    (1, 0, 0), (-1, 0, 0), (0, 1, 0), (0, -1, 0), (0, 0, 1), (0, 0, -1),
    (1, 1, 0), (-1, -1, 0), (1, -1, 0), (-1, 1, 0),
    (1, 0, 1), (-1, 0, -1), (1, 0, -1), (-1, 0, 1),
    (0, 1, 1), (0, -1, -1), (0, 1, -1), (0, -1, 1),
]
ORDER = [0, 3, 4, 5, 6, 15, 16, 17, 18, 1, 7, 9, 11, 13, 2, 8, 10, 12, 14]
POS = [ORDER.index(i) for i in range(19)]
X_START = {1: 9, -1: 14}
Y_GROUP = {1: [3, 7, 10, 15, 17], -1: [4, 8, 9, 16, 18]}
CORNERS = [(1, 1), (-1, -1), (1, -1), (-1, 1)]
CORNER_POP = {(1, 1): 7, (-1, -1): 8, (1, -1): 9, (-1, 1): 10}
PLANES = (7, 11, 15)
RATE2, RATE3, RATE4 = 1.25, 1.5, 1.4


Node = namedtuple("Node", [
    "pops", "porosity", "adj", "porous", "walls", "out", "gap", "speed", "late_sens", "early_sens",
    "ahead", "behind",
])


def split_planes(f):
    out = []
    for start in PLANES:
        a, b, c, d = f[start : start + 4]
        s1, s2, t1, t2 = a + b, c + d, a - b, c - d
        out.append((s1 + s2, s1 - s2, t1 + t2, t1 - t2, t1, t2))
    return out


def split_faces(f):
    return [f[1] + f[2], f[3] + f[4], f[5] + f[6]], [f[1] - f[2], f[3] - f[4], f[5] - f[6]]


def nonequilibrium(f):
    (w_xy, w_xz, w_yz) = planes = split_planes(f)
    sums, diffs = split_faces(f)
    second = [sums[0] + w_xy[0] + w_xz[0], sums[1] + w_xy[0] + w_yz[0], sums[2] + w_xz[0] + w_yz[0]]
    jx = diffs[0] + (w_xy[2] + w_xz[2])
    jy = diffs[1] + (w_xy[3] + w_yz[2])
    jz = diffs[2] + (w_xz[3] + w_yz[3])
    rho = (f[0] + sums[0]) + (sums[1] + sums[2]) + ((w_xy[0] + w_xz[0]) + w_yz[0])
    inverse = 1.0 / rho
    ux, uy, uz = jx * inverse, jy * inverse, jz * inverse
    qx, qy, qz = jx * ux, jy * uy, jz * uz
    third_rho = rho * (1.0 / 3.0)
    second = [second[0] - third_rho - qx, second[1] - third_rho - qy, second[2] - third_rho - qz]
    product = [w_xy[1] - jx * uy, w_xz[1] - jx * uz, w_yz[1] - jy * uz]
    kx, ky, kz = jx * (1.0 / 3.0), jy * (1.0 / 3.0), jz * (1.0 / 3.0)
    first = [w_xy[2] - kx, w_xz[2] - kx, w_yz[2] - ky]
    other = [w_xy[3] - ky, w_xz[3] - kz, w_yz[3] - kz]
    base = rho * (1.0 / 9.0) + ((qx + qy) + qz) * (1.0 / 3.0)
    fourth = [w_xy[0] - base + 0.5 * qz, w_xz[0] - base + 0.5 * qy, w_yz[0] - base + 0.5 * qx]
    return planes, diffs, (ux, uy, uz), (second, product, first, other, fourth)


def forward(f, phi):
    _, _, u, (second, product, first, other, fourth) = nonequilibrium(f)
    second = [v * (0.5 * RATE2) for v in second]
    product = [v * (0.25 * RATE2) for v in product]
    first = [v * (0.25 * RATE3) for v in first]
    other = [v * (0.25 * RATE3) for v in other]
    fourth = [v * (0.25 * RATE4) for v in fourth]
    change = [None] * 19
    change[0] = 4.0 * (fourth[0] + fourth[1] + fourth[2]) - 2.0 * (second[0] + second[1] + second[2])
    evens = [
        second[0] - 2.0 * (fourth[0] + fourth[1]),
        second[1] - 2.0 * (fourth[0] + fourth[2]),
        second[2] - 2.0 * (fourth[1] + fourth[2]),
    ]
    odds = [
        2.0 * (first[0] + first[1]),
        2.0 * (other[0] + first[2]),
        2.0 * (other[1] + other[2]),
    ]
    for axis in range(3):
        change[1 + 2 * axis] = evens[axis] - odds[axis]
        change[2 + 2 * axis] = evens[axis] + odds[axis]
    for plane, start in enumerate(PLANES):
        h, k = fourth[plane] + product[plane], fourth[plane] - product[plane]
        p, q = first[plane] + other[plane], first[plane] - other[plane]
        change[start : start + 4] = [h + p, h - p, k + q, k - q]
    relaxed = [f[i] - change[i] for i in range(19)]
    opposite = [0] + [i + 1 if i % 2 else i - 1 for i in range(1, 19)]
    gap = [f[opposite[i]] - relaxed[i] for i in range(19)]
    return [relaxed[i] + phi * gap[i] for i in range(19)], gap, u


def adjoint_moments(a):
    a_planes = split_planes(a)
    a_sums, a_diffs = split_faces(a)
    half = [0.5 * v for v in a_sums]
    n_xy, n_xz, n_yz = a_planes
    b2 = [RATE2 * (v - a[0]) for v in half]
    b11 = [(0.25 * RATE2) * n[1] for n in a_planes]
    hx, hy, hz = [(0.5 * RATE3) * v for v in a_diffs]
    b_first = [
        (0.25 * RATE3) * n_xy[2] - hx, (0.25 * RATE3) * n_xz[2] - hx, (0.25 * RATE3) * n_yz[2] - hy
    ]
    b_other = [
        (0.25 * RATE3) * n_xy[3] - hy, (0.25 * RATE3) * n_xz[3] - hz, (0.25 * RATE3) * n_yz[3] - hz
    ]
    b4 = [
        RATE4 * (0.25 * n_xy[0] - (half[0] + half[1]) + a[0]),
        RATE4 * (0.25 * n_xz[0] - (half[0] + half[2]) + a[0]),
        RATE4 * (0.25 * n_yz[0] - (half[1] + half[2]) + a[0]),
    ]
    return a_planes, a_diffs, (b2, b11, b_first, b_other, b4)


def fraction_cotangent(f_planes, f_diffs, moments, a_planes, a_diffs, b):
    parts = []
    for mine, theirs in zip(b, moments):
        part = None
        for v, m in zip(mine, theirs):
            part = v * m if part is None else part + v * m
        parts.append(part)
    for axis in range(3):
        parts[axis] = parts[axis] - f_diffs[axis] * a_diffs[axis]
    for k, (p, n) in enumerate(zip(f_planes, a_planes)):
        parts[k + 2] = parts[k + 2] - p[4] * n[4] - p[5] * n[5]
    return ((parts[0] + parts[1]) + (parts[2] + parts[3])) + parts[4]


def population_cotangent(u, a, b, phi):
    ux, uy, uz = u
    b2, b11, b_first, b_other, b4 = b
    keep = 1.0 - phi
    b2, b11, b_first, b_other, b4 = [
        [keep * v for v in part] for part in (b2, b11, b_first, b_other, b4)
    ]
    total4 = b4[0] + b4[1] + b4[2]
    twice = total4 * (2.0 / 3.0)
    cx, cy, cz = 2.0 * b2[0] + twice - b4[2], 2.0 * b2[1] + twice - b4[1], 2.0 * b2[2] + twice - b4[0]
    wx = cx * ux + b11[0] * uy + b11[1] * uz
    wy = cy * uy + b11[0] * ux + b11[2] * uz
    wz = cz * uz + b11[1] * ux + b11[2] * uy
    r0 = (
        0.5 * (ux * wx + uy * wy + uz * wz)
        - (b2[0] + b2[1] + b2[2]) * (1.0 / 3.0)
        - total4 * (1.0 / 9.0)
    )
    rx = -(b_first[0] + b_first[1]) * (1.0 / 3.0) - wx
    ry = -(b_other[0] + b_first[2]) * (1.0 / 3.0) - wy
    rz = -(b_other[1] + b_other[2]) * (1.0 / 3.0) - wz
    result = [None] * 19
    result[0] = a[0] - r0
    evens = [r0 + b2[0], r0 + b2[1], r0 + b2[2]]
    for axis, odd in enumerate((rx, ry, rz)):
        back = phi * (a[1 + 2 * axis] - a[2 + 2 * axis]) + odd
        result[1 + 2 * axis] = (a[1 + 2 * axis] - evens[axis]) - back
        result[2 + 2 * axis] = (a[2 + 2 * axis] - evens[axis]) + back
    for plane, (start, one, two) in enumerate(((7, 0, 1), (11, 0, 2), (15, 1, 2))):
        even = evens[one] + b2[two] + b4[plane]
        p = (rx, ry, rz)[one] + b_first[plane]
        q = (rx, ry, rz)[two] + b_other[plane]
        h, k = even + b11[plane], even - b11[plane]
        s = (p + q) + phi * (a[start] - a[start + 1])
        t = (p - q) + phi * (a[start + 2] - a[start + 3])
        result[start] = (a[start] - h) - s
        result[start + 1] = (a[start + 1] - h) + s
        result[start + 2] = (a[start + 2] - k) - t
        result[start + 3] = (a[start + 3] - k) + t
    return result


def kernel(
    sizes, pops_hbm, porosity_hbm, adj_hbm, porous_hbm, walls_hbm, owners_hbm, slots_hbm,
    out, gathered,
    pops, porosity, adj, porous, walls, owners, slots, gap, speed, ahead, behind,
    late_sens, early_sens, y_send, y_recv, c_send, c_recv, message, names,
    load_sem, halo_send, halo_recv, patch_send, patch_recv,
):
    n_gx, n_gy, cx, cy, nz = sizes
    n = n_gx * n_gy
    stride = cy + 16
    gx, gy = lax.axis_index("gx"), lax.axis_index("gy")

    faces = [pl.ds(0, cy), pl.ds((cx - 1) * cy, cy)]
    middle = pl.ds(cy, (cx - 2) * cy)
    pairs = [(porosity_hbm, porosity), (porous_hbm, porous), (walls_hbm, walls)]
    pairs += [(pops_hbm.at[:, part, :], pops.at[:, part, :]) for part in faces + [middle]]
    pairs += [(adj_hbm, adj), (owners_hbm, owners), (slots_hbm, slots)]
    loads = [
        pltpu.make_async_copy(src, dst, load_sem.at[k]) for k, (src, dst) in enumerate(pairs)
    ]
    for load in loads:
        load.start()

    def near(dx, dy):
        x, y = gx + dx, gy + dy
        return (
            jnp.where(x >= n_gx, x - n_gx, jnp.where(x < 0, x + n_gx, x)),
            jnp.where(y >= n_gy, y - n_gy, jnp.where(y < 0, y + n_gy, y)),
        )

    def for_others(act):
        for dy in range(1, n_gy):
            act(0, dy)

        @pl.loop(1, n_gx)
        def _(dx):
            for dy in range(n_gy):
                act(dx, dy)

    barrier = pltpu.get_barrier_semaphore()
    for_others(lambda dx, dy: pl.semaphore_signal(
        barrier, inc=1, device_id=near(dx, dy), device_id_type=MESH
    ))

    def spin(value, shift):
        return value if shift == 0 else pltpu.roll(value, shift % nz, 1)

    def window(x, y, along_x):
        return pl.ds(x * cy + y, 8, stride=cy) if along_x else pl.ds(x * cy + y, 8)

    def shifted(x, y, i, sign, along_x):
        ex, ey, _ = VELOCITIES[i]
        row = (x + 1 - sign * ex) * stride + 8 + y - sign * ey
        return pl.ds(row, 8, stride=stride) if along_x else pl.ds(row, 8)

    def padded(x, y, along_x):
        row = (x + 1) * stride + 8 + y
        return pl.ds(row, 8, stride=stride) if along_x else pl.ds(row, 8)

    whole = Node(
        pops, porosity, adj, porous, walls, out, gap, speed, late_sens, early_sens, ahead, behind
    )

    def layer(x, count):
        plain = pl.ds(pl.multiple_of(x * cy, cy), count * cy)
        wide = pl.ds(pl.multiple_of(x * stride, stride), (count + 2) * stride)
        parts = [
            ref.at[plain, :] if len(ref.shape) == 2 else ref.at[:, plain, :] for ref in whole[:10]
        ]
        return Node(*parts, ahead.at[:, wide, :], behind.at[:, wide, :])

    def fractions(node, rows):
        porous_here = node.porous[rows, :].astype(jnp.float32)
        wall = node.walls[rows, :] == 1
        phi = jnp.where(wall, 1.0, porous_here * node.porosity[rows, :])
        return phi, jnp.where(wall, 0.0, porous_here)

    def pack(stage, values, x, y, sign):
        side = 1 if y else -1
        which = 0 if side > 0 else 1
        for k, i in enumerate(Y_GROUP[side * sign]):
            y_send[stage, which, k, pl.ds(pl.multiple_of(x, 8), 8), :] = values[i]

    def step_one(node, x, y, along_x, at=0):
        rows = window(x, y, along_x)
        f = [node.pops[i, rows, :] for i in range(19)]
        phi, _ = fractions(node, rows)
        values, apart, u = forward(f, phi)
        values = [spin(v, VELOCITIES[i][2]) for i, v in enumerate(values)]
        if along_x:
            pack(0, values, at, y, 1)
        else:
            for i in range(19):
                node.ahead[POS[i], padded(x, y, False), :] = values[i]
                node.gap[i, rows, :] = apart[i]
            for axis in range(3):
                node.speed[axis, rows, :] = u[axis]

    def step_two(node, x, y, along_x, at=0):
        rows = window(x, y, along_x)
        f = [node.ahead[POS[i], shifted(x, y, i, 1, along_x), :] for i in range(19)]
        phi, weight = fractions(node, rows)
        f_planes, f_diffs, u, moments = nonequilibrium(f)
        a_planes, a_diffs, b = adjoint_moments([node.adj[i, rows, :] for i in range(19)])
        sens = fraction_cotangent(f_planes, f_diffs, moments, a_planes, a_diffs, b)
        node.late_sens[rows, :] = weight * sens
        values = population_cotangent(u, [node.adj[i, rows, :] for i in range(19)], b, phi)
        values = [spin(v, -VELOCITIES[i][2]) for i, v in enumerate(values)]
        if along_x:
            pack(1, values, at, y, -1)
        for i in range(19):
            node.behind[POS[i], padded(x, y, along_x), :] = values[i]

    def pulled(node, x, y, along_x):
        return [node.behind[POS[i], shifted(x, y, i, -1, along_x), :] for i in range(19)]

    def step_sens(node, x, y, along_x, at=0):
        rows = window(x, y, along_x)
        a = pulled(node, x, y, along_x)
        parts = [a[i] * node.gap[i, rows, :] for i in range(4)]
        for i in range(4, 19):
            parts[i % 4] = parts[i % 4] + a[i] * node.gap[i, rows, :]
        _, weight = fractions(node, rows)
        node.early_sens[rows, :] = weight * ((parts[0] + parts[1]) + (parts[2] + parts[3]))

    def step_out(node, x, y, along_x, at=0):
        rows = window(x, y, along_x)
        phi, _ = fractions(node, rows)
        _, _, b = adjoint_moments(pulled(node, x, y, along_x))
        u = [node.speed[axis, rows, :] for axis in range(3)]
        values = population_cotangent(u, pulled(node, x, y, along_x), b, phi)
        for i in range(19):
            node.out[i, rows, :] = values[i]

    def y_edges(step, stop):
        for y in (0, cy - 1):
            @pl.loop(0, stop // 8)
            def _(part):
                step(layer(part * 8, 8), 0, y, True, part * 8)

    def x_faces(step):
        for x in (0, cx - 1):
            for y in range(0, cy, 8):
                step(whole, x, y, False)

    def inner(step, start, stop):
        @pl.loop(start, stop)
        def _(x):
            node = layer(x, 1)
            for y in range(0, cy, 8):
                step(node, 0, y, False)

    def send(stage, number, src, dst, dx, dy):
        copy = pltpu.make_async_remote_copy(
            src_ref=src, dst_ref=dst,
            send_sem=halo_send.at[stage, number], recv_sem=halo_recv.at[stage, number],
            device_id=near(dx, dy), device_id_type=MESH,
        )
        copy.start()
        return copy

    def send_y(stage, sign):
        for number, (sx, sy) in enumerate(CORNERS):
            k = Y_GROUP[sy * sign].index(CORNER_POP[(sx * sign, sy * sign)])
            row = pl.ds(cx - 1 if sx > 0 else 0, 1)
            c_send[stage, number, :, :] = y_send[stage, 0 if sy > 0 else 1, k, row, :]
        copies = [
            send(stage, which, y_send.at[stage, which], y_recv.at[stage, which], 0, side)
            for which, side in enumerate((1, -1))
        ]
        for number, (sx, sy) in enumerate(CORNERS):
            copies.append(
                send(stage, 2 + number, c_send.at[stage, number], c_recv.at[stage, number], sx, sy)
            )
        return copies

    def send_x(stage, buffer, sign):
        copies = []
        for which, side in enumerate((1, -1)):
            group = pl.ds(X_START[side * sign], 5)
            source = (cx if side > 0 else 1) * stride + 8
            target = (0 if side > 0 else cx + 1) * stride + 8
            copies.append(send(
                stage, 6 + which, buffer.at[group, pl.ds(source, cy), :],
                buffer.at[group, pl.ds(target, cy), :], side, 0,
            ))
        return copies

    def receive(stage, copies, buffer, sign):
        for copy in copies:
            copy.wait_recv()
        for which, side in enumerate((1, -1)):
            row = 8 + (-1 if side > 0 else cy)
            for k, i in enumerate(Y_GROUP[side * sign]):
                for x in range(0, cx, 8):
                    buffer[POS[i], pl.ds((x + 1) * stride + row, 8, stride=stride), :] = (
                        y_recv[stage, which, k, pl.ds(x, 8), :]
                    )
        for number, (sx, sy) in enumerate(CORNERS):
            i = CORNER_POP[(sx * sign, sy * sign)]
            row = (0 if sx > 0 else cx + 1) * stride + 8 + (-1 if sy > 0 else cy)
            buffer[POS[i], pl.ds(row, 1), :] = c_recv[stage, number]

    names[...] = jnp.zeros_like(names)
    for load in loads[:6]:
        load.wait()
    y_edges(step_one, cx)
    pl.semaphore_wait(barrier, n - 1)
    copies = send_y(0, 1)
    x_faces(step_one)
    copies += send_x(0, ahead, 1)
    inner(step_one, 1, cx - 1)
    for load in loads[6:]:
        load.wait()
    names[pl.ds(0, 1), pl.ds(0, owners.shape[1])] = (
        owners[...] * PATCH_DEV + slots[...]
    ).astype(jnp.float32)
    inner(step_two, 1, cx // 2)
    receive(0, copies, ahead, 1)
    y_edges(step_two, cx)
    later = send_y(1, -1)
    x_faces(step_two)
    later += send_x(1, behind, -1)
    inner(step_two, cx // 2, cx - 1)
    inner(step_sens, 1, cx - 1)
    inner(step_out, 1, cx // 2)
    receive(1, later, behind, -1)
    y_edges(step_sens, cx)
    x_faces(step_sens)

    rows_of = []
    for x in range(0, cx, 2):
        part = None
        for start in (x * cy, x * cy + 1, (x + 1) * cy, (x + 1) * cy + 1):
            for sens in (late_sens, early_sens):
                piece = sens[pl.ds(start, cy // 2, stride=2), :]
                part = piece if part is None else part + piece
        rows_of.append(part)
    blocks = (cx // 2) * (cy // 2)
    rows_of.append(jnp.zeros((nz - blocks, nz), jnp.float32))
    contract = (((1,), (1,)), ((), ()))
    ones = jnp.ones((8, nz), jnp.float32)
    sums = lax.dot_general(
        ones, jnp.concatenate(rows_of, axis=0), contract,
        precision=lax.Precision.HIGHEST, preferred_element_type=jnp.float32,
    )
    note = sums[0:1, :] + pltpu.roll(names[...], nz // 2, 1)[0:1, :]
    message[0] = note
    gathered[0] = note

    for_others(lambda dx, dy: pltpu.make_async_remote_copy(
        src_ref=message.at[0], dst_ref=gathered.at[dx * n_gy + dy],
        send_sem=patch_send, recv_sem=patch_recv,
        device_id=near(dx, dy), device_id_type=MESH,
    ).start())

    y_edges(step_out, cx // 2)
    x_faces(step_out)
    inner(step_out, cx // 2, cx - 1)

    for copy in copies + later:
        copy.wait_send()
    others = gathered.at[pl.ds(1, n - 1)]
    pltpu.make_async_copy(others, others, patch_recv).wait()
    pltpu.make_async_copy(others, others, patch_send).wait()


def finish(sizes, result, gathered, out_hbm, patch_hbm, patch_ref, store_sem):
    n_gx, n_gy, _, _, nz = sizes
    n = n_gx * n_gy
    parts = [pl.ds(0, 10), pl.ds(10, 9)]
    stores = [
        pltpu.make_async_copy(result.at[part], out_hbm.at[part], store_sem.at[k])
        for k, part in enumerate(parts)
    ]
    for store in stores:
        store.start()
    me = lax.axis_index("gx") * n_gy + lax.axis_index("gy")
    lane = lax.broadcasted_iota(jnp.int32, (1, nz), 1)
    low = lane < nz // 2
    patch = lax.broadcasted_iota(jnp.int32, (PATCH_DEV, nz), 0).astype(jnp.float32)
    base = (me * PATCH_DEV).astype(jnp.float32)

    def add(k, total):
        one, two = gathered[k], gathered[k + n // 2]
        one_turned, two_turned = pltpu.roll(one, nz // 2, 1), pltpu.roll(two, nz // 2, 1)
        values = jnp.where(low, one, two_turned)
        names = jnp.where(low, one_turned, two) - base
        return total + jnp.where(names == patch, values, 0.0)

    total = jnp.zeros((PATCH_DEV, nz), jnp.float32)
    total = lax.fori_loop(0, n // 2, add, total, unroll=8)
    summed = lax.dot_general(
        jnp.ones((8, nz), jnp.float32), total, (((1,), (1,)), ((), ())),
        precision=lax.Precision.HIGHEST, preferred_element_type=jnp.float32,
    )
    patch_ref[...] = summed[0:1, :]
    stores.append(pltpu.make_async_copy(patch_ref, patch_hbm, store_sem.at[2]))
    stores[-1].start()
    for store in stores:
        store.wait()


def body(sizes, populations, porosity, adjoint_in, porous, walls, owners, slots):
    _, cx, cy, nz = populations.shape
    rows = cx * cy
    n = sizes[0] * sizes[1]
    flat = lambda v: v.reshape(v.shape[:-3] + (rows, nz))
    row = lambda v: v.reshape(1, -1)
    hbm = pl.BlockSpec(memory_space=pltpu.HBM)
    vmem = pl.BlockSpec(memory_space=pltpu.VMEM)
    wide = (19, (cx + 2) * (cy + 16), nz)
    f32 = jnp.float32
    whole = jax.ShapeDtypeStruct((19, rows, nz), f32)
    shape = (*sizes, cx, cy, nz)
    blocks = slots.shape[-1]
    arguments = [flat(v) for v in (populations, porosity, adjoint_in, porous, walls)]
    arguments += [row(owners), row(slots)]
    result, gathered = pl.pallas_call(
        partial(kernel, shape),
        out_shape=(whole, jax.ShapeDtypeStruct((n, 1, nz), f32)),
        in_specs=[hbm] * 7,
        out_specs=(vmem, vmem),
        scratch_shapes=[
            pltpu.VMEM((19, rows, nz), f32),
            pltpu.VMEM((rows, nz), f32),
            pltpu.VMEM((19, rows, nz), f32),
            pltpu.VMEM((rows, nz), jnp.int32),
            pltpu.VMEM((rows, nz), jnp.int32),
            pltpu.VMEM((1, blocks), jnp.int32),
            pltpu.VMEM((1, blocks), jnp.int32),
            pltpu.VMEM((19, rows, nz), f32),
            pltpu.VMEM((3, rows, nz), f32),
            pltpu.VMEM(wide, f32),
            pltpu.VMEM(wide, f32),
            pltpu.VMEM((rows, nz), f32),
            pltpu.VMEM((rows, nz), f32),
            pltpu.VMEM((2, 2, 5, cx, nz), f32),
            pltpu.VMEM((2, 2, 5, cx, nz), f32),
            pltpu.VMEM((2, 4, 1, nz), f32),
            pltpu.VMEM((2, 4, 1, nz), f32),
            pltpu.VMEM((1, 1, nz), f32),
            pltpu.VMEM((8, nz), f32),
            pltpu.SemaphoreType.DMA((9,)),
            pltpu.SemaphoreType.DMA((2, 8)),
            pltpu.SemaphoreType.DMA((2, 8)),
            pltpu.SemaphoreType.DMA,
            pltpu.SemaphoreType.DMA,
        ],
        compiler_params=pltpu.CompilerParams(
            collective_id=0, has_side_effects=True, vmem_limit_bytes=40 * 1024 * 1024
        ),
    )(
        *[pltpu.with_memory_space_constraint(v, pltpu.HBM) for v in arguments]
    )
    adjoint_out, patch = pl.pallas_call(
        partial(finish, shape),
        out_shape=(whole, jax.ShapeDtypeStruct((1, PATCH_DEV), f32)),
        in_specs=[vmem, vmem],
        out_specs=(hbm, hbm),
        scratch_shapes=[pltpu.VMEM((1, PATCH_DEV), f32), pltpu.SemaphoreType.DMA((3,))],
        compiler_params=pltpu.CompilerParams(vmem_limit_bytes=16 * 1024 * 1024),
    )(result, gathered)
    return adjoint_out.reshape(populations.shape), patch.reshape(-1)


def solution(mesh):
    sizes = (mesh.shape["gx"], mesh.shape["gy"])
    return jax.shard_map(
        partial(body, sizes),
        mesh=mesh,
        in_specs=(
            P(None, "gx", "gy", None),
            P("gx", "gy", None),
            P(None, "gx", "gy", None),
            P("gx", "gy", None),
            P("gx", "gy", None),
            P("gx", "gy", None, None),
            P("gx", "gy", None),
        ),
        out_specs=(P(None, "gx", "gy", None), P(("gx", "gy"))),
        check_vma=False,
    )
```

```python
from collections import namedtuple
from functools import partial

import jax
import jax.numpy as jnp
from jax import lax
from jax.experimental import pallas as pl
from jax.experimental.pallas import tpu as pltpu
from jax.sharding import PartitionSpec as P

PATCH_DEV = 256
MESH = pl.DeviceIdType.MESH

VELOCITIES = [
    (0, 0, 0),
    (1, 0, 0), (-1, 0, 0), (0, 1, 0), (0, -1, 0), (0, 0, 1), (0, 0, -1),
    (1, 1, 0), (-1, -1, 0), (1, -1, 0), (-1, 1, 0),
    (1, 0, 1), (-1, 0, -1), (1, 0, -1), (-1, 0, 1),
    (0, 1, 1), (0, -1, -1), (0, 1, -1), (0, -1, 1),
]
ORDER = [0, 3, 4, 5, 6, 15, 16, 17, 18, 1, 7, 9, 11, 13, 2, 8, 10, 12, 14]
POS = [ORDER.index(i) for i in range(19)]
X_START = {1: 9, -1: 14}
Y_GROUP = {1: [3, 7, 10, 15, 17], -1: [4, 8, 9, 16, 18]}
CORNERS = [(1, 1), (-1, -1), (1, -1), (-1, 1)]
CORNER_POP = {(1, 1): 7, (-1, -1): 8, (1, -1): 9, (-1, 1): 10}
PLANES = (7, 11, 15)
RATE2, RATE3, RATE4 = 1.25, 1.5, 1.4


Node = namedtuple("Node", [
    "pops", "porosity", "adj", "porous", "walls", "out", "gap", "speed", "late_sens", "early_sens",
    "ahead", "behind",
])


def split_planes(f):
    out = []
    for start in PLANES:
        a, b, c, d = f[start : start + 4]
        s1, s2, t1, t2 = a + b, c + d, a - b, c - d
        out.append((s1 + s2, s1 - s2, t1 + t2, t1 - t2, t1, t2))
    return out


def split_faces(f):
    return [f[1] + f[2], f[3] + f[4], f[5] + f[6]], [f[1] - f[2], f[3] - f[4], f[5] - f[6]]


def nonequilibrium(f):
    (w_xy, w_xz, w_yz) = planes = split_planes(f)
    sums, diffs = split_faces(f)
    second = [sums[0] + w_xy[0] + w_xz[0], sums[1] + w_xy[0] + w_yz[0], sums[2] + w_xz[0] + w_yz[0]]
    jx = diffs[0] + (w_xy[2] + w_xz[2])
    jy = diffs[1] + (w_xy[3] + w_yz[2])
    jz = diffs[2] + (w_xz[3] + w_yz[3])
    rho = (f[0] + sums[0]) + (sums[1] + sums[2]) + ((w_xy[0] + w_xz[0]) + w_yz[0])
    inverse = 1.0 / rho
    ux, uy, uz = jx * inverse, jy * inverse, jz * inverse
    qx, qy, qz = jx * ux, jy * uy, jz * uz
    third_rho = rho * (1.0 / 3.0)
    second = [second[0] - third_rho - qx, second[1] - third_rho - qy, second[2] - third_rho - qz]
    product = [w_xy[1] - jx * uy, w_xz[1] - jx * uz, w_yz[1] - jy * uz]
    kx, ky, kz = jx * (1.0 / 3.0), jy * (1.0 / 3.0), jz * (1.0 / 3.0)
    first = [w_xy[2] - kx, w_xz[2] - kx, w_yz[2] - ky]
    other = [w_xy[3] - ky, w_xz[3] - kz, w_yz[3] - kz]
    base = rho * (1.0 / 9.0) + ((qx + qy) + qz) * (1.0 / 3.0)
    fourth = [w_xy[0] - base + 0.5 * qz, w_xz[0] - base + 0.5 * qy, w_yz[0] - base + 0.5 * qx]
    return planes, diffs, (ux, uy, uz), (second, product, first, other, fourth)


def forward(f, phi):
    _, _, u, (second, product, first, other, fourth) = nonequilibrium(f)
    second = [v * (0.5 * RATE2) for v in second]
    product = [v * (0.25 * RATE2) for v in product]
    first = [v * (0.25 * RATE3) for v in first]
    other = [v * (0.25 * RATE3) for v in other]
    fourth = [v * (0.25 * RATE4) for v in fourth]
    change = [None] * 19
    change[0] = 4.0 * (fourth[0] + fourth[1] + fourth[2]) - 2.0 * (second[0] + second[1] + second[2])
    evens = [
        second[0] - 2.0 * (fourth[0] + fourth[1]),
        second[1] - 2.0 * (fourth[0] + fourth[2]),
        second[2] - 2.0 * (fourth[1] + fourth[2]),
    ]
    odds = [
        2.0 * (first[0] + first[1]),
        2.0 * (other[0] + first[2]),
        2.0 * (other[1] + other[2]),
    ]
    for axis in range(3):
        change[1 + 2 * axis] = evens[axis] - odds[axis]
        change[2 + 2 * axis] = evens[axis] + odds[axis]
    for plane, start in enumerate(PLANES):
        h, k = fourth[plane] + product[plane], fourth[plane] - product[plane]
        p, q = first[plane] + other[plane], first[plane] - other[plane]
        change[start : start + 4] = [h + p, h - p, k + q, k - q]
    relaxed = [f[i] - change[i] for i in range(19)]
    opposite = [0] + [i + 1 if i % 2 else i - 1 for i in range(1, 19)]
    gap = [f[opposite[i]] - relaxed[i] for i in range(19)]
    return [relaxed[i] + phi * gap[i] for i in range(19)], gap, u


def adjoint_moments(a):
    a_planes = split_planes(a)
    a_sums, a_diffs = split_faces(a)
    half = [0.5 * v for v in a_sums]
    n_xy, n_xz, n_yz = a_planes
    b2 = [RATE2 * (v - a[0]) for v in half]
    b11 = [(0.25 * RATE2) * n[1] for n in a_planes]
    hx, hy, hz = [(0.5 * RATE3) * v for v in a_diffs]
    b_first = [
        (0.25 * RATE3) * n_xy[2] - hx, (0.25 * RATE3) * n_xz[2] - hx, (0.25 * RATE3) * n_yz[2] - hy
    ]
    b_other = [
        (0.25 * RATE3) * n_xy[3] - hy, (0.25 * RATE3) * n_xz[3] - hz, (0.25 * RATE3) * n_yz[3] - hz
    ]
    b4 = [
        RATE4 * (0.25 * n_xy[0] - (half[0] + half[1]) + a[0]),
        RATE4 * (0.25 * n_xz[0] - (half[0] + half[2]) + a[0]),
        RATE4 * (0.25 * n_yz[0] - (half[1] + half[2]) + a[0]),
    ]
    return a_planes, a_diffs, (b2, b11, b_first, b_other, b4)


def fraction_cotangent(f_planes, f_diffs, moments, a_planes, a_diffs, b):
    parts = []
    for mine, theirs in zip(b, moments):
        part = None
        for v, m in zip(mine, theirs):
            part = v * m if part is None else part + v * m
        parts.append(part)
    for axis in range(3):
        parts[axis] = parts[axis] - f_diffs[axis] * a_diffs[axis]
    for k, (p, n) in enumerate(zip(f_planes, a_planes)):
        parts[k + 2] = parts[k + 2] - p[4] * n[4] - p[5] * n[5]
    return ((parts[0] + parts[1]) + (parts[2] + parts[3])) + parts[4]


def population_cotangent(u, a, b, phi):
    ux, uy, uz = u
    b2, b11, b_first, b_other, b4 = b
    keep = 1.0 - phi
    b2, b11, b_first, b_other, b4 = [
        [keep * v for v in part] for part in (b2, b11, b_first, b_other, b4)
    ]
    total4 = b4[0] + b4[1] + b4[2]
    twice = total4 * (2.0 / 3.0)
    cx, cy, cz = 2.0 * b2[0] + twice - b4[2], 2.0 * b2[1] + twice - b4[1], 2.0 * b2[2] + twice - b4[0]
    wx = cx * ux + b11[0] * uy + b11[1] * uz
    wy = cy * uy + b11[0] * ux + b11[2] * uz
    wz = cz * uz + b11[1] * ux + b11[2] * uy
    r0 = (
        0.5 * (ux * wx + uy * wy + uz * wz)
        - (b2[0] + b2[1] + b2[2]) * (1.0 / 3.0)
        - total4 * (1.0 / 9.0)
    )
    rx = -(b_first[0] + b_first[1]) * (1.0 / 3.0) - wx
    ry = -(b_other[0] + b_first[2]) * (1.0 / 3.0) - wy
    rz = -(b_other[1] + b_other[2]) * (1.0 / 3.0) - wz
    result = [None] * 19
    result[0] = a[0] - r0
    evens = [r0 + b2[0], r0 + b2[1], r0 + b2[2]]
    for axis, odd in enumerate((rx, ry, rz)):
        back = phi * (a[1 + 2 * axis] - a[2 + 2 * axis]) + odd
        result[1 + 2 * axis] = (a[1 + 2 * axis] - evens[axis]) - back
        result[2 + 2 * axis] = (a[2 + 2 * axis] - evens[axis]) + back
    for plane, (start, one, two) in enumerate(((7, 0, 1), (11, 0, 2), (15, 1, 2))):
        even = evens[one] + b2[two] + b4[plane]
        p = (rx, ry, rz)[one] + b_first[plane]
        q = (rx, ry, rz)[two] + b_other[plane]
        h, k = even + b11[plane], even - b11[plane]
        s = (p + q) + phi * (a[start] - a[start + 1])
        t = (p - q) + phi * (a[start + 2] - a[start + 3])
        result[start] = (a[start] - h) - s
        result[start + 1] = (a[start + 1] - h) + s
        result[start + 2] = (a[start + 2] - k) - t
        result[start + 3] = (a[start + 3] - k) + t
    return result


def kernel(
    sizes, pops_hbm, porosity_hbm, adj_hbm, porous_hbm, walls_hbm, owners_hbm, slots_hbm,
    out, gathered,
    pops, porosity, adj, porous, walls, owners, slots, gap, speed, ahead, behind,
    late_sens, early_sens, y_send, y_recv, c_send, c_recv, message, names,
    load_sem, halo_send, halo_recv, patch_send, patch_recv,
):
    n_gx, n_gy, cx, cy, nz = sizes
    n = n_gx * n_gy
    stride = cy + 16
    gx, gy = lax.axis_index("gx"), lax.axis_index("gy")

    pairs = [(pops_hbm, pops), (porosity_hbm, porosity), (porous_hbm, porous), (walls_hbm, walls)]
    pairs += [(adj_hbm, adj), (owners_hbm, owners), (slots_hbm, slots)]
    loads = [
        pltpu.make_async_copy(src, dst, load_sem.at[k]) for k, (src, dst) in enumerate(pairs)
    ]
    for load in loads:
        load.start()

    def near(dx, dy):
        x, y = gx + dx, gy + dy
        return (
            jnp.where(x >= n_gx, x - n_gx, jnp.where(x < 0, x + n_gx, x)),
            jnp.where(y >= n_gy, y - n_gy, jnp.where(y < 0, y + n_gy, y)),
        )

    def for_others(act):
        for dy in range(1, n_gy):
            act(0, dy)

        @pl.loop(1, n_gx)
        def _(dx):
            for dy in range(n_gy):
                act(dx, dy)

    barrier = pltpu.get_barrier_semaphore()
    for_others(lambda dx, dy: pl.semaphore_signal(
        barrier, inc=1, device_id=near(dx, dy), device_id_type=MESH
    ))

    def spin(value, shift):
        return value if shift == 0 else pltpu.roll(value, shift % nz, 1)

    def window(x, y, along_x):
        return pl.ds(x * cy + y, 8, stride=cy) if along_x else pl.ds(x * cy + y, 8)

    def shifted(x, y, i, sign, along_x):
        ex, ey, _ = VELOCITIES[i]
        row = (x + 1 - sign * ex) * stride + 8 + y - sign * ey
        return pl.ds(row, 8, stride=stride) if along_x else pl.ds(row, 8)

    def padded(x, y, along_x):
        row = (x + 1) * stride + 8 + y
        return pl.ds(row, 8, stride=stride) if along_x else pl.ds(row, 8)

    whole = Node(
        pops, porosity, adj, porous, walls, out, gap, speed, late_sens, early_sens, ahead, behind
    )

    def layer(x, count):
        plain = pl.ds(pl.multiple_of(x * cy, cy), count * cy)
        wide = pl.ds(pl.multiple_of(x * stride, stride), (count + 2) * stride)
        parts = [
            ref.at[plain, :] if len(ref.shape) == 2 else ref.at[:, plain, :] for ref in whole[:10]
        ]
        return Node(*parts, ahead.at[:, wide, :], behind.at[:, wide, :])

    def fractions(node, rows):
        porous_here = node.porous[rows, :].astype(jnp.float32)
        wall = node.walls[rows, :] == 1
        phi = jnp.where(wall, 1.0, porous_here * node.porosity[rows, :])
        return phi, jnp.where(wall, 0.0, porous_here)

    def pack(stage, values, x, y, sign):
        side = 1 if y else -1
        which = 0 if side > 0 else 1
        for k, i in enumerate(Y_GROUP[side * sign]):
            y_send[stage, which, k, pl.ds(pl.multiple_of(x, 8), 8), :] = values[i]

    def step_one(node, x, y, along_x, at=0):
        rows = window(x, y, along_x)
        f = [node.pops[i, rows, :] for i in range(19)]
        phi, _ = fractions(node, rows)
        values, apart, u = forward(f, phi)
        values = [spin(v, VELOCITIES[i][2]) for i, v in enumerate(values)]
        if along_x:
            pack(0, values, at, y, 1)
        else:
            for i in range(19):
                node.ahead[POS[i], padded(x, y, False), :] = values[i]
                node.gap[i, rows, :] = apart[i]
            for axis in range(3):
                node.speed[axis, rows, :] = u[axis]

    def step_two(node, x, y, along_x, at=0):
        rows = window(x, y, along_x)
        f = [node.ahead[POS[i], shifted(x, y, i, 1, along_x), :] for i in range(19)]
        phi, weight = fractions(node, rows)
        f_planes, f_diffs, u, moments = nonequilibrium(f)
        a_planes, a_diffs, b = adjoint_moments([node.adj[i, rows, :] for i in range(19)])
        sens = fraction_cotangent(f_planes, f_diffs, moments, a_planes, a_diffs, b)
        node.late_sens[rows, :] = weight * sens
        values = population_cotangent(u, [node.adj[i, rows, :] for i in range(19)], b, phi)
        values = [spin(v, -VELOCITIES[i][2]) for i, v in enumerate(values)]
        if along_x:
            pack(1, values, at, y, -1)
        for i in range(19):
            node.behind[POS[i], padded(x, y, along_x), :] = values[i]

    def pulled(node, x, y, along_x):
        return [node.behind[POS[i], shifted(x, y, i, -1, along_x), :] for i in range(19)]

    def step_sens(node, x, y, along_x, at=0):
        rows = window(x, y, along_x)
        a = pulled(node, x, y, along_x)
        parts = [a[i] * node.gap[i, rows, :] for i in range(4)]
        for i in range(4, 19):
            parts[i % 4] = parts[i % 4] + a[i] * node.gap[i, rows, :]
        _, weight = fractions(node, rows)
        node.early_sens[rows, :] = weight * ((parts[0] + parts[1]) + (parts[2] + parts[3]))

    def step_out(node, x, y, along_x, at=0):
        rows = window(x, y, along_x)
        phi, _ = fractions(node, rows)
        _, _, b = adjoint_moments(pulled(node, x, y, along_x))
        u = [node.speed[axis, rows, :] for axis in range(3)]
        values = population_cotangent(u, pulled(node, x, y, along_x), b, phi)
        for i in range(19):
            node.out[i, rows, :] = values[i]

    def y_edges(step, stop):
        for y in (0, cy - 1):
            @pl.loop(0, stop // 8)
            def _(part):
                step(layer(part * 8, 8), 0, y, True, part * 8)

    def x_faces(step):
        for x in (0, cx - 1):
            for y in range(0, cy, 8):
                step(whole, x, y, False)

    def inner(step, start, stop):
        @pl.loop(start, stop)
        def _(x):
            node = layer(x, 1)
            for y in range(0, cy, 8):
                step(node, 0, y, False)

    def send(stage, number, src, dst, dx, dy):
        copy = pltpu.make_async_remote_copy(
            src_ref=src, dst_ref=dst,
            send_sem=halo_send.at[stage, number], recv_sem=halo_recv.at[stage, number],
            device_id=near(dx, dy), device_id_type=MESH,
        )
        copy.start()
        return copy

    def send_y(stage, sign):
        for number, (sx, sy) in enumerate(CORNERS):
            k = Y_GROUP[sy * sign].index(CORNER_POP[(sx * sign, sy * sign)])
            row = pl.ds(cx - 1 if sx > 0 else 0, 1)
            c_send[stage, number, :, :] = y_send[stage, 0 if sy > 0 else 1, k, row, :]
        copies = [
            send(stage, which, y_send.at[stage, which], y_recv.at[stage, which], 0, side)
            for which, side in enumerate((1, -1))
        ]
        for number, (sx, sy) in enumerate(CORNERS):
            copies.append(
                send(stage, 2 + number, c_send.at[stage, number], c_recv.at[stage, number], sx, sy)
            )
        return copies

    def send_x(stage, buffer, sign):
        copies = []
        for which, side in enumerate((1, -1)):
            group = pl.ds(X_START[side * sign], 5)
            source = (cx if side > 0 else 1) * stride + 8
            target = (0 if side > 0 else cx + 1) * stride + 8
            copies.append(send(
                stage, 6 + which, buffer.at[group, pl.ds(source, cy), :],
                buffer.at[group, pl.ds(target, cy), :], side, 0,
            ))
        return copies

    def receive(stage, copies, buffer, sign):
        for copy in copies:
            copy.wait_recv()
        for which, side in enumerate((1, -1)):
            row = 8 + (-1 if side > 0 else cy)
            for k, i in enumerate(Y_GROUP[side * sign]):
                for x in range(0, cx, 8):
                    buffer[POS[i], pl.ds((x + 1) * stride + row, 8, stride=stride), :] = (
                        y_recv[stage, which, k, pl.ds(x, 8), :]
                    )
        for number, (sx, sy) in enumerate(CORNERS):
            i = CORNER_POP[(sx * sign, sy * sign)]
            row = (0 if sx > 0 else cx + 1) * stride + 8 + (-1 if sy > 0 else cy)
            buffer[POS[i], pl.ds(row, 1), :] = c_recv[stage, number]

    names[...] = jnp.zeros_like(names)
    for load in loads[:4]:
        load.wait()
    y_edges(step_one, cx)
    pl.semaphore_wait(barrier, n - 1)
    copies = send_y(0, 1)
    x_faces(step_one)
    copies += send_x(0, ahead, 1)
    inner(step_one, 1, cx - 1)
    for load in loads[4:]:
        load.wait()
    names[pl.ds(0, 1), pl.ds(0, owners.shape[1])] = (
        owners[...] * PATCH_DEV + slots[...]
    ).astype(jnp.float32)
    inner(step_two, 1, cx // 2)
    receive(0, copies, ahead, 1)
    y_edges(step_two, cx)
    later = send_y(1, -1)
    x_faces(step_two)
    later += send_x(1, behind, -1)
    inner(step_two, cx // 2, cx - 1)
    inner(step_sens, 1, cx - 1)
    inner(step_out, 1, cx // 2)
    receive(1, later, behind, -1)
    y_edges(step_sens, cx)
    x_faces(step_sens)

    rows_of = []
    for x in range(0, cx, 2):
        part = None
        for start in (x * cy, x * cy + 1, (x + 1) * cy, (x + 1) * cy + 1):
            for sens in (late_sens, early_sens):
                piece = sens[pl.ds(start, cy // 2, stride=2), :]
                part = piece if part is None else part + piece
        rows_of.append(part)
    blocks = (cx // 2) * (cy // 2)
    rows_of.append(jnp.zeros((nz - blocks, nz), jnp.float32))
    sums = jnp.sum(jnp.concatenate(rows_of, axis=0).T, axis=0, keepdims=True)
    note = sums + pltpu.roll(names[...], nz // 2, 1)[0:1, :]
    message[0] = note
    gathered[0] = note

    for_others(lambda dx, dy: pltpu.make_async_remote_copy(
        src_ref=message.at[0], dst_ref=gathered.at[dx * n_gy + dy],
        send_sem=patch_send, recv_sem=patch_recv,
        device_id=near(dx, dy), device_id_type=MESH,
    ).start())

    y_edges(step_out, cx // 2)
    x_faces(step_out)
    inner(step_out, cx // 2, cx - 1)

    for copy in copies + later:
        copy.wait_send()
    others = gathered.at[pl.ds(1, n - 1)]
    pltpu.make_async_copy(others, others, patch_recv).wait()
    pltpu.make_async_copy(others, others, patch_send).wait()


def finish(sizes, result, gathered, out_hbm, patch_hbm, patch_ref, store_sem):
    n_gx, n_gy, _, _, nz = sizes
    n = n_gx * n_gy
    parts = [pl.ds(0, 10), pl.ds(10, 9)]
    stores = [
        pltpu.make_async_copy(result.at[part], out_hbm.at[part], store_sem.at[k])
        for k, part in enumerate(parts)
    ]
    for store in stores:
        store.start()
    me = lax.axis_index("gx") * n_gy + lax.axis_index("gy")
    lane = lax.broadcasted_iota(jnp.int32, (1, nz), 1)
    low = lane < nz // 2
    patch = lax.broadcasted_iota(jnp.int32, (PATCH_DEV, nz), 0).astype(jnp.float32)
    base = (me * PATCH_DEV).astype(jnp.float32)

    def add(k, total):
        one, two = gathered[k], gathered[k + n // 2]
        one_turned, two_turned = pltpu.roll(one, nz // 2, 1), pltpu.roll(two, nz // 2, 1)
        values = jnp.where(low, one, two_turned)
        names = jnp.where(low, one_turned, two) - base
        return total + jnp.where(names == patch, values, 0.0)

    total = jnp.zeros((PATCH_DEV, nz), jnp.float32)
    total = lax.fori_loop(0, n // 2, add, total, unroll=8)
    summed = lax.dot_general(
        jnp.ones((8, nz), jnp.float32), total, (((1,), (1,)), ((), ())),
        precision=lax.Precision.HIGHEST, preferred_element_type=jnp.float32,
    )
    patch_ref[...] = summed[0:1, :]
    stores.append(pltpu.make_async_copy(patch_ref, patch_hbm, store_sem.at[2]))
    stores[-1].start()
    for store in stores:
        store.wait()


def body(sizes, populations, porosity, adjoint_in, porous, walls, owners, slots):
    _, cx, cy, nz = populations.shape
    rows = cx * cy
    n = sizes[0] * sizes[1]
    flat = lambda v: v.reshape(v.shape[:-3] + (rows, nz))
    row = lambda v: v.reshape(1, -1)
    hbm = pl.BlockSpec(memory_space=pltpu.HBM)
    vmem = pl.BlockSpec(memory_space=pltpu.VMEM)
    wide = (19, (cx + 2) * (cy + 16), nz)
    f32 = jnp.float32
    whole = jax.ShapeDtypeStruct((19, rows, nz), f32)
    shape = (*sizes, cx, cy, nz)
    blocks = slots.shape[-1]
    arguments = [flat(v) for v in (populations, porosity, adjoint_in, porous, walls)]
    arguments += [row(owners), row(slots)]
    result, gathered = pl.pallas_call(
        partial(kernel, shape),
        out_shape=(whole, jax.ShapeDtypeStruct((n, 1, nz), f32)),
        in_specs=[hbm] * 7,
        out_specs=(vmem, vmem),
        scratch_shapes=[
            pltpu.VMEM((19, rows, nz), f32),
            pltpu.VMEM((rows, nz), f32),
            pltpu.VMEM((19, rows, nz), f32),
            pltpu.VMEM((rows, nz), jnp.int32),
            pltpu.VMEM((rows, nz), jnp.int32),
            pltpu.VMEM((1, blocks), jnp.int32),
            pltpu.VMEM((1, blocks), jnp.int32),
            pltpu.VMEM((19, rows, nz), f32),
            pltpu.VMEM((3, rows, nz), f32),
            pltpu.VMEM(wide, f32),
            pltpu.VMEM(wide, f32),
            pltpu.VMEM((rows, nz), f32),
            pltpu.VMEM((rows, nz), f32),
            pltpu.VMEM((2, 2, 5, cx, nz), f32),
            pltpu.VMEM((2, 2, 5, cx, nz), f32),
            pltpu.VMEM((2, 4, 1, nz), f32),
            pltpu.VMEM((2, 4, 1, nz), f32),
            pltpu.VMEM((1, 1, nz), f32),
            pltpu.VMEM((8, nz), f32),
            pltpu.SemaphoreType.DMA((7,)),
            pltpu.SemaphoreType.DMA((2, 8)),
            pltpu.SemaphoreType.DMA((2, 8)),
            pltpu.SemaphoreType.DMA,
            pltpu.SemaphoreType.DMA,
        ],
        compiler_params=pltpu.CompilerParams(
            collective_id=0, has_side_effects=True, vmem_limit_bytes=40 * 1024 * 1024
        ),
    )(
        *[pltpu.with_memory_space_constraint(v, pltpu.HBM) for v in arguments]
    )
    adjoint_out, patch = pl.pallas_call(
        partial(finish, shape),
        out_shape=(whole, jax.ShapeDtypeStruct((1, PATCH_DEV), f32)),
        in_specs=[vmem, vmem],
        out_specs=(hbm, hbm),
        scratch_shapes=[pltpu.VMEM((1, PATCH_DEV), f32), pltpu.SemaphoreType.DMA((3,))],
        compiler_params=pltpu.CompilerParams(vmem_limit_bytes=16 * 1024 * 1024),
    )(result, gathered)
    return adjoint_out.reshape(populations.shape), patch.reshape(-1)


def solution(mesh):
    sizes = (mesh.shape["gx"], mesh.shape["gy"])
    return jax.shard_map(
        partial(body, sizes),
        mesh=mesh,
        in_specs=(
            P(None, "gx", "gy", None),
            P("gx", "gy", None),
            P(None, "gx", "gy", None),
            P("gx", "gy", None),
            P("gx", "gy", None),
            P("gx", "gy", None, None),
            P("gx", "gy", None),
        ),
        out_specs=(P(None, "gx", "gy", None), P(("gx", "gy"))),
        check_vma=False,
    )
```
